512 devices in a mesh: lat: 16 (over x, y), lon: 32 (over z, core).
Axes of the slice: x: 4, y: 4, z: 16, core: 2. Of those that a mesh axis runs over, the one named last changes fastest.
Arguments:
- wind_u: float32 [32, 128, 4096], P(None, 'lat', 'lon'), may hold values from -6 to 6
- wind_v: float32 [32, 128, 4096], P(None, 'lat', 'lon'), may hold values from -6 to 6
Outputs:
- modes: float32 [32, 2, 128, 4096], P(None, None, 'lat', 'lon')
- factor: float32 [32, 32], replicated
The draws below stay inside these ranges and needn't reach their ends.
All inputs are finite; a program needn't handle non-finite values.
Results may differ from the reference program's by a relative error of at most 0.0003.
Values sent between devices are 32-bit elements; how exact they have to be, the bound alone decides.
No kernel may reach another device: no remote copies, remote signals or barrier semaphores. Data moves between devices by JAX's collectives and lax.ppermute only.
A program may use at most 64 MiB of HBM per device.

```python
import math
import jax
import jax.numpy as jnp
from jax import lax

SNAPS = 32
NLAT = 128
NLON = 4096
ROWS = 1048576


def wind_field(key, offset):
    keys = [jax.random.fold_in(key, offset + number) for number in range(4)]
    lat_frac = jnp.arange(NLAT).astype(jnp.float32) / NLAT
    lon_frac = jnp.arange(NLON).astype(jnp.float32) / NLON
    noise = jax.random.normal(keys[0], (SNAPS, NLAT, NLON), jnp.float32)
    ramp = 3.0 ** (0.5 * lat_frac[:, None] + 0.5 * lon_frac[None, :])
    base = jax.random.uniform(keys[1], (NLAT, NLON), jnp.float32, -1.2, 1.2)
    cells = jnp.exp(jax.random.uniform(keys[2], (NLAT, NLON), jnp.float32, 0.0, math.log(3.4)))
    raw_snaps = jnp.exp(jax.random.uniform(keys[3], (SNAPS, 1, 1), jnp.float32, 0.0, math.log(10.0)))
    snaps = raw_snaps / jnp.min(raw_snaps)
    field = 0.025 * snaps * (ramp * cells)[None, :, :] * (base[None, :, :] + noise / 30.0)
    return jnp.clip(field, -6.0, 6.0)


def draw_wind_u(key, part):
    return wind_field(key, 100)


def draw_wind_v(key, part):
    return wind_field(key, 200)


def setup_inputs(seed: int = 0) -> dict:
    seeds = jax.random.split(jax.random.key(seed), 3)
    wind_u = draw_wind_u(jax.random.fold_in(seeds[2], 71), 0)
    wind_v = draw_wind_v(jax.random.fold_in(seeds[2], 71), 0)
    return {"wind_u": wind_u, "wind_v": wind_v}


def upper_factor(gram):
    count = gram.shape[0]
    positions = jnp.arange(count)

    def column_step(k, state):
        rest, lower = state
        onehot = (positions == k).astype(jnp.float32)
        below = (positions >= k).astype(jnp.float32)
        pivot = jnp.sum(rest * onehot[:, None] * onehot[None, :])
        column = lax.optimization_barrier(jnp.sum(rest * onehot[None, :], axis=1)) * below / jnp.sqrt(pivot)
        lower = lower + column[:, None] * onehot[None, :]
        rest = rest - column[:, None] * column[None, :]
        return (rest, lower)
    start = (gram.astype(jnp.float32), jnp.zeros(gram.shape, jnp.float32))
    rest, lower = lax.fori_loop(0, count, column_step, start)
    return lower.T

def inverse_upper(upper):
    count = upper.shape[0]
    positions = jnp.arange(count)

    def row_step(i, result):
        k = count - 1 - i
        onehot = (positions == k).astype(jnp.float32)
        row_of = lax.optimization_barrier(jnp.sum(upper * onehot[:, None], axis=0))
        diag = jnp.sum(row_of * onehot)
        off_diag = row_of * (1.0 - onehot)
        new_row = (onehot - lax.optimization_barrier(jnp.sum(off_diag[:, None] * result, axis=0))) / diag
        return result + onehot[:, None] * new_row[None, :]
    return lax.fori_loop(0, count, row_step, jnp.zeros(upper.shape, jnp.float32))

def build_columns(wind_u, wind_v):
    step = 2.0 * math.pi / NLON
    index = jnp.arange(NLAT).astype(jnp.float32)
    cosines = jnp.cos((index + 0.5 - NLAT / 2) * step)
    weight_c = cosines[None, :, None]

    def lat_diff(field):
        padded = jnp.pad(field * weight_c, ((0, 0), (1, 1), (0, 0)))
        return padded[:, 2:, :] - padded[:, :-2, :]

    def lon_diff(field):
        return jnp.roll(field, -1, axis=2) - jnp.roll(field, 1, axis=2)
    scale = (0.5 / jnp.sqrt(cosines))[None, :, None]
    vorticity = (lon_diff(wind_v) - lat_diff(wind_u)) * scale
    divergence = (lon_diff(wind_u) + lat_diff(wind_v)) * scale
    return jnp.stack([vorticity, divergence], axis=1)

def reference(wind_u, wind_v):
    highest = lax.Precision.HIGHEST
    block = build_columns(wind_u, wind_v).reshape(SNAPS, -1)
    gram_one = jnp.dot(block, block.T, precision=highest, preferred_element_type=jnp.float32)
    first = upper_factor(gram_one)
    solved = jnp.dot(inverse_upper(first).T, block, precision=highest, preferred_element_type=jnp.float32)
    gram_two = jnp.dot(solved, solved.T, precision=highest, preferred_element_type=jnp.float32)
    second = upper_factor(gram_two)
    root = math.sqrt(ROWS)
    modes = jnp.dot(inverse_upper(second).T, solved, precision=highest, preferred_element_type=jnp.float32) * root
    factor = jnp.dot(second, first, precision=highest, preferred_element_type=jnp.float32) / root
    return (modes.reshape(SNAPS, 2, NLAT, NLON), factor)
```

```python
import functools
import math

import jax
import jax.numpy as jnp
from jax import lax
from jax.experimental import pallas as pl
from jax.experimental.pallas import tpu as pltpu
from jax.sharding import Mesh, PartitionSpec as P

SNAPS = 32
ROWS = 8
LANES = 128
CHUNKS = 2 * ROWS
X_PARTS = 4
G_PARTS = 5


def two_sum(a, b):
    total = a + b
    part = total - a
    return total, (a - (total - part)) + (b - part)


def pair_add(a, b):
    total, error = two_sum(a[0], b[0])
    error = error + (a[1] + b[1])
    high = total + error
    return high, error - (high - total)


def pair_tree(pairs):
    while len(pairs) > 1:
        merged = [pair_add(a, b) for a, b in zip(pairs[::2], pairs[1::2])]
        pairs = merged + pairs[len(merged) * 2 :]
    return pairs[0]


def split_parts(value, low, bound, count):
    parts = []
    grid = bound * 2.0**17
    for index in range(count):
        part = (value + grid) - grid
        parts.append(part.astype(jnp.bfloat16))
        value = value - part
        if low is not None and index == 2:
            value = value + low
        grid = grid * 2.0**-8
    return parts


def lane_iota(shape):
    return lax.broadcasted_iota(jnp.int32, shape, 1)


def row_iota(shape):
    return lax.broadcasted_iota(jnp.int32, shape, 0)


def edge_picker():
    shape = (8, LANES)
    row, lane = row_iota(shape), lane_iota(shape)
    first = jnp.logical_and(row == 0, lane == 0)
    last = jnp.logical_and(row == 1, lane == LANES - 1)
    return jnp.where(jnp.logical_or(first, last), 1.0, 0.0).astype(jnp.float32)


def tile_row(ref, index):
    return ref[pl.ds(index, SNAPS, stride=ROWS), :]


def pack_kernel(u_ref, v_ref, north_ref, south_ref, west_ref, east_ref):
    rows = [tile_row(ref, i) for ref in (u_ref, v_ref) for i in range(ROWS)]
    north_ref[:SNAPS, :] = rows[0]
    north_ref[SNAPS:, :] = rows[ROWS]
    south_ref[:SNAPS, :] = rows[ROWS - 1]
    south_ref[SNAPS:, :] = rows[2 * ROWS - 1]
    sides = lax.dot_general(
        edge_picker(),
        jnp.concatenate(rows, axis=0),
        (((1,), (1,)), ((), ())),
        precision=lax.Precision.HIGHEST,
        preferred_element_type=jnp.float32,
    )
    west_ref[...] = sides[0:1, :]
    east_ref[...] = sides[1:2, :]


def fold_parts(blocks, count):
    total = None
    for part in reversed(range(count)):
        tile, group = divmod(part, 4)
        pair = tuple(block[:, tile * LANES : (tile + 1) * LANES] for block in blocks)
        if group:
            pair = tuple(pltpu.roll(block, LANES - 32 * group, 1) for block in pair)
        total = pair if total is None else pair_add(total, pair)
    return total


def gram_kernel(u_ref, v_ref, low_lat_ref, high_lat_ref, low_lon_ref, high_lon_ref, table_ref, parts_ref, gram_ref, x_ref):
    shape = (SNAPS, LANES)
    lane = lane_iota(shape)
    wide = (8, CHUNKS * SNAPS)
    row = row_iota(wide)
    edges = jnp.where(row == 0, low_lon_ref[...], jnp.where(row == 1, high_lon_ref[...], 0.0))
    beyond = lax.dot_general(
        edges,
        edge_picker(),
        (((0,), (0,)), ((), ())),
        precision=lax.Precision.HIGHEST,
        preferred_element_type=jnp.float32,
    )

    def lon_diff(field, value, i):
        outer = beyond[(field * ROWS + i) * SNAPS : (field * ROWS + i + 1) * SNAPS, :]
        after = jnp.where(lane == LANES - 1, outer, pltpu.roll(value, LANES - 1, 1))
        before = jnp.where(lane == 0, outer, pltpu.roll(value, 1, 1))
        return after - before

    def wind(ref, field, i):
        if i < 0:
            return low_lat_ref[field * SNAPS : (field + 1) * SNAPS, :]
        if i >= ROWS:
            return high_lat_ref[field * SNAPS : (field + 1) * SNAPS, :]
        return tile_row(ref, i)

    def lat_diff(ref, field, i):
        return table_ref[i + 2 : i + 3, :] * wind(ref, field, i + 1) - table_ref[i : i + 1, :] * wind(ref, field, i - 1)

    largest = jnp.zeros(shape, jnp.float32)
    for i in range(ROWS):
        scale = table_ref[16 + i : 17 + i, :]
        vorticity = (lon_diff(1, wind(v_ref, 1, i), i) - lat_diff(u_ref, 0, i)) * scale
        divergence = (lon_diff(0, wind(u_ref, 0, i), i) + lat_diff(v_ref, 1, i)) * scale
        x_ref[i] = vorticity
        x_ref[ROWS + i] = divergence
        largest = jnp.maximum(largest, jnp.maximum(jnp.abs(vorticity), jnp.abs(divergence)))
    bound = jnp.broadcast_to(jnp.max(largest, axis=1, keepdims=True), shape)
    for chunk in range(CHUNKS):
        for part, value in enumerate(split_parts(x_ref[chunk], None, bound, X_PARTS)):
            parts_ref[part * SNAPS : (part + 1) * SNAPS, chunk * LANES : (chunk + 1) * LANES] = value
    size = X_PARTS * SNAPS
    high, low = jnp.zeros((size, size), jnp.float32), jnp.zeros((size, size), jnp.float32)
    for chunk in range(CHUNKS // 2):
        piece = parts_ref[:, chunk * 2 * LANES : (chunk + 1) * 2 * LANES]
        product = lax.dot_general(
            piece, piece, (((1,), (1,)), ((), ())), preferred_element_type=jnp.float32
        )
        high, error = two_sum(high, product)
        low = low + error
    total = None
    for part in reversed(range(X_PARTS)):
        rows = slice(part * SNAPS, (part + 1) * SNAPS)
        pair = (high[rows], low[rows])
        total = pair if total is None else pair_add(total, pair)
    pair = fold_parts(total, X_PARTS)
    packed = jnp.concatenate([pack_lanes(pair[0]), pack_lanes(pair[1])], axis=0)
    for copy in range(gram_ref.shape[0]):
        gram_ref[copy] = packed


def pack_lanes(square):
    lane = lane_iota((8, LANES))
    packed = square[0:8]
    for group in range(1, 4):
        moved = pltpu.roll(square[8 * group : 8 * group + 8], 32 * group, 1)
        packed = jnp.where(lane >= 32 * group, moved, packed)
    return packed


def unpack_lanes(packed):
    lane = lane_iota((8, LANES))
    rows = [packed] + [pltpu.roll(packed, LANES - 32 * group, 1) for group in range(1, 4)]
    return jnp.concatenate([jnp.where(lane < 32, row, 0.0) for row in rows], axis=0)


def add_pairs(ref):
    return pair_tree([(ref[k, 0:8, :], ref[k, 8:16, :]) for k in range(ref.shape[0])])


def merge_kernel(all_ref, out_ref):
    packed = jnp.concatenate(add_pairs(all_ref), axis=0)
    for copy in range(out_ref.shape[0]):
        out_ref[copy] = packed


def factor_and_inverse(square):
    shape = (8, LANES)
    lane, row = lane_iota(shape), row_iota(shape)
    blocks = [
        jnp.where(lane == row + (32 + 8 * b), 1.0, square[8 * b : 8 * b + 8]) for b in range(4)
    ]
    pivots = [jnp.ones(shape, jnp.float32) for _ in range(4)]

    def spread_lane(value, k):
        return jnp.broadcast_to(value[:, k : k + 1], shape)

    def spread_row(value, k):
        return jnp.broadcast_to(value[k : k + 1, :], shape)

    for k in range(0, SNAPS, 2):
        b, j = divmod(k, 8)
        first = [spread_lane(block, k) for block in blocks[b:]]
        second = [spread_lane(block, k + 1) for block in blocks[b:]]
        row0 = spread_row(blocks[b], j)
        row1 = spread_row(blocks[b], j + 1)
        pivot0 = spread_row(first[0], j)
        below = spread_row(first[0], j + 1)
        beside = spread_row(second[0], j)
        corner = spread_row(second[0], j + 1)
        inverse0 = 1.0 / pivot0
        ratio = below * inverse0
        row1 = row1 - ratio * row0
        pivot1 = corner - ratio * beside
        inverse1 = 1.0 / pivot1
        for index in range(b, 4):
            left = first[index - b] * inverse0
            right = (second[index - b] - left * beside) * inverse1
            new = blocks[index] - left * row0 - right * row1
            if index == b:
                new = jnp.where(row > j + 1, new, blocks[b])
                new = jnp.where(row == j + 1, row1, new)
            blocks[index] = new
        pivots[b] = jnp.where(row == j, pivot0, jnp.where(row == j + 1, pivot1, pivots[b]))
    upper, lower = [], []
    for b in range(4):
        scale = lax.rsqrt(pivots[b])
        scale = scale * (1.5 - 0.5 * pivots[b] * scale * scale)
        scaled = blocks[b] * scale
        upper.append(jnp.where(jnp.logical_and(lane >= row + 8 * b, lane < 32), scaled, 0.0))
        lower.append(jnp.where(lane < 32, pltpu.roll(scaled, LANES - 32, 1), 0.0))
    return jnp.concatenate(upper, axis=0), jnp.concatenate(lower, axis=0)


def product_of_parts(left, right):
    count = len(right)
    tiles = -(-count // 4)
    rows = jnp.concatenate(left, axis=0)
    columns = jnp.concatenate(list(right) + [jnp.zeros_like(right[0])] * (4 * tiles - count), axis=0)
    blocks = lax.dot_general(
        rows, columns, (((1,), (1,)), ((), ())), preferred_element_type=jnp.float32
    )
    total = None
    for part in reversed(range(len(left))):
        value = blocks[part * SNAPS : (part + 1) * SNAPS, :]
        pair = (value, jnp.zeros_like(value))
        total = pair if total is None else pair_add(total, pair)
    lane = lane_iota((SNAPS, LANES))
    return tuple(jnp.where(lane < 32, value, 0.0) for value in fold_parts(total, count))


def row_bound(value):
    return jnp.broadcast_to(jnp.max(jnp.abs(value), axis=1, keepdims=True), value.shape)


def exact_dot(left, right, contract):
    return lax.dot_general(
        left,
        right,
        (contract, ((), ())),
        precision=lax.Precision.HIGHEST,
        preferred_element_type=jnp.float32,
    )


def modes_kernel(root, all_ref, parts_ref, modes_ref, factor_ref):
    high, low = add_pairs(all_ref)
    high, low = unpack_lanes(high), unpack_lanes(low)
    first, first_inverse = factor_and_inverse(high)
    gram_parts = [p[:, :32] for p in split_parts(high, low, row_bound(high), G_PARTS)]
    inverse_parts = [p[:, :32] for p in split_parts(first_inverse, None, row_bound(first_inverse), X_PARTS)]
    half = product_of_parts(inverse_parts, gram_parts)
    half_parts = [p[:, :32] for p in split_parts(half[0], half[1], row_bound(half[0]), G_PARTS)]
    second_gram = product_of_parts(half_parts, inverse_parts)[0]
    second, second_inverse = factor_and_inverse(second_gram)
    factor_ref[...] = exact_dot(second[:, :32], first[:, :32], ((1,), (0,))) * (1.0 / root)
    weights = exact_dot(second_inverse[:, :32], first_inverse[:, :32], ((1,), (0,))) * root
    weights = jnp.concatenate([weights] * 4, axis=1)
    pieces = []
    for _ in range(3):
        piece = weights.astype(jnp.bfloat16)
        pieces.append(piece)
        weights = weights - piece.astype(jnp.float32)
    stacked = jnp.concatenate(pieces, axis=0)
    for chunk in range(CHUNKS // 2):
        product = jnp.dot(
            stacked,
            parts_ref[:, chunk * 2 * LANES : (chunk + 1) * 2 * LANES],
            preferred_element_type=jnp.float32,
        )
        value = (product[64:96] + product[32:64]) + product[0:32]
        for side in range(2):
            modes_ref[pl.ds(2 * chunk + side, SNAPS, stride=CHUNKS), :] = value[:, side * LANES : (side + 1) * LANES]


def on_chip(count):
    return [pl.BlockSpec(memory_space=pltpu.VMEM)] * count


def call(kernel, shapes, operands, scratch=()):
    return pl.pallas_call(
        kernel,
        out_shape=shapes,
        in_specs=on_chip(len(operands)),
        out_specs=on_chip(len(shapes)),
        scratch_shapes=list(scratch),
    )(*operands)


def shards(wind_u, wind_v):
    f32 = functools.partial(jax.ShapeDtypeStruct, dtype=jnp.float32)
    lat_axis, lon_axis = "lat", ("z", "core")
    lat_count, lon_count = lax.axis_size(lat_axis), lax.axis_size(lon_axis)
    near, far = lax.axis_size((lat_axis, "core")), lax.axis_size("z")
    u = wind_u.reshape(SNAPS * ROWS, LANES)
    v = wind_v.reshape(SNAPS * ROWS, LANES)

    with jax.named_scope("halo"):
        rows, column = f32((2 * SNAPS, LANES)), f32((1, CHUNKS * SNAPS))
        north, south, west, east = call(pack_kernel, [rows, rows, column, column], (u, v))
        up = [(i, i + 1) for i in range(lat_count - 1)]
        around = [(i, (i + 1) % lon_count) for i in range(lon_count)]
        back = lambda pairs: [(target, source) for source, target in pairs]
        low_lat = lax.ppermute(south, lat_axis, up)
        high_lat = lax.ppermute(north, lat_axis, back(up))
        low_lon = lax.ppermute(east, lon_axis, around)
        high_lon = lax.ppermute(west, lon_axis, back(around))

    with jax.named_scope("table"):
        step = 2.0 * math.pi / (lon_count * LANES)
        line = row_iota((24, LANES))
        first_row = lax.axis_index(lat_axis) * ROWS
        index = (first_row + jnp.where(line < 16, line - 1, line - 16)).astype(jnp.float32)
        cosine = jnp.cos((index + 0.5 - lat_count * ROWS / 2) * step)
        table = jnp.where(line < 16, cosine, 0.5 / jnp.sqrt(cosine))

    with jax.named_scope("gram"):
        parts_shape = jax.ShapeDtypeStruct((X_PARTS * SNAPS, CHUNKS * LANES), jnp.bfloat16)
        parts, gram = call(
            gram_kernel,
            [parts_shape, f32((near, 16, LANES))],
            (u, v, low_lat, high_lat, low_lon, high_lon, table),
            [pltpu.VMEM((CHUNKS, SNAPS, LANES), jnp.float32)],
        )

    with jax.named_scope("sum_near"):
        gathered = lax.all_to_all(gram, (lat_axis, "core"), 0, 0, tiled=True)
        (gram,) = call(merge_kernel, [f32((far, 16, LANES))], (gathered,))
    with jax.named_scope("sum_far"):
        gathered = lax.all_to_all(gram, "z", 0, 0, tiled=True)

    with jax.named_scope("modes"):
        root = math.sqrt(lat_count * lon_count * CHUNKS * LANES)
        modes, factor = call(
            functools.partial(modes_kernel, root),
            [f32((SNAPS * CHUNKS, LANES)), f32((SNAPS, SNAPS))],
            (gathered, parts),
        )
    return modes.reshape(SNAPS, 2, ROWS, LANES), factor


def solution(mesh):
    lat_count, lon_count = mesh.devices.shape
    inner = Mesh(mesh.devices.reshape(lat_count, lon_count // 2, 2), ("lat", "z", "core"))
    spec = P(None, "lat", ("z", "core"))
    return jax.shard_map(
        shards,
        mesh=inner,
        in_specs=(spec, spec),
        out_specs=(P(None, None, "lat", ("z", "core")), P()),
        check_vma=False,
    )
```

```python
import functools
import math

import jax
import jax.numpy as jnp
from jax import lax
from jax.experimental import pallas as pl
from jax.experimental.pallas import tpu as pltpu
from jax.sharding import Mesh, PartitionSpec as P

SNAPS = 32
ROWS = 8
LANES = 128
CHUNKS = 2 * ROWS
X_PARTS = 4
G_PARTS = 5
PACKED = 9
EDGES = (0, ROWS - 1)
INNER = tuple(range(1, ROWS - 1))


def two_sum(a, b):
    total = a + b
    part = total - a
    return total, (a - (total - part)) + (b - part)


def pair_add(a, b):
    total, error = two_sum(a[0], b[0])
    error = error + (a[1] + b[1])
    high = total + error
    return high, error - (high - total)


def split_parts(value, low, bound, count):
    parts = []
    grid = bound * 2.0**17
    for index in range(count):
        part = (value + grid) - grid
        parts.append(part.astype(jnp.bfloat16))
        value = value - part
        if low is not None and index == 2:
            value = value + low
        grid = grid * 2.0**-8
    return parts


def lane_iota(shape):
    return lax.broadcasted_iota(jnp.int32, shape, 1)


def row_iota(shape):
    return lax.broadcasted_iota(jnp.int32, shape, 0)


def edge_picker():
    shape = (8, LANES)
    row, lane = row_iota(shape), lane_iota(shape)
    first = jnp.logical_and(row == 0, lane == 0)
    last = jnp.logical_and(row == 1, lane == LANES - 1)
    return jnp.where(jnp.logical_or(first, last), 1.0, 0.0).astype(jnp.float32)


def tile_row(ref, index):
    return ref[pl.ds(index, SNAPS, stride=ROWS), :]


def rows_kernel(u_ref, v_ref, north_ref, south_ref):
    for field, ref in enumerate((u_ref, v_ref)):
        place = slice(field * SNAPS, (field + 1) * SNAPS)
        north_ref[place, :] = tile_row(ref, 0)
        south_ref[place, :] = tile_row(ref, ROWS - 1)


def sides_kernel(u_ref, v_ref, west_ref, east_ref):
    rows = [tile_row(ref, i) for i in range(ROWS) for ref in (u_ref, v_ref)]
    sides = exact_dot(edge_picker(), jnp.concatenate(rows, axis=0), ((1,), (1,)))
    west_ref[...] = sides[0:1, :]
    east_ref[...] = sides[1:2, :]


def fold_parts(blocks, count):
    total = None
    for part in reversed(range(count)):
        tile, group = divmod(part, 4)
        pair = tuple(block[:, tile * LANES : (tile + 1) * LANES] for block in blocks)
        if group:
            pair = tuple(pltpu.roll(block, LANES - 32 * group, 1) for block in pair)
        total = pair if total is None else pair_add(total, pair)
    return total


def cut_and_multiply(winds, lat_halos, lon_halos, table_ref, rows, parts_ref, x_ref):
    shape = (SNAPS, LANES)
    lane = lane_iota(shape)
    low, high = lon_halos[0][...], lon_halos[1][...]
    if rows == EDGES:
        left = lane_iota((1, LANES)) < LANES // 2
        low, high = (jnp.where(left, side[:, :LANES], side[:, -LANES:]) for side in (low, high))
        starts = {0: 0, ROWS - 1: 2 * SNAPS}
    else:
        starts = {i: 2 * SNAPS * i for i in rows}
    row = row_iota((8, low.shape[1]))
    edges = jnp.where(row == 0, low, jnp.where(row == 1, high, 0.0))
    beyond = exact_dot(edges, edge_picker(), ((0,), (0,)))

    def lon_diff(field, i):
        value = tile_row(winds[field], i)
        start = starts[i] + field * SNAPS
        outer = beyond[start : start + SNAPS, :]
        after = jnp.where(lane == LANES - 1, outer, pltpu.roll(value, LANES - 1, 1))
        before = jnp.where(lane == 0, outer, pltpu.roll(value, 1, 1))
        return after - before

    def weighted(field, i):
        if 0 <= i < ROWS:
            value = tile_row(winds[field], i)
        else:
            value = lat_halos[i >= ROWS][field * SNAPS : (field + 1) * SNAPS, :]
        return table_ref[i + 1 : i + 2, :] * value

    def lat_diff(field, i):
        return weighted(field, i + 1) - weighted(field, i - 1)

    largest = jnp.zeros(shape, jnp.float32)
    for index, i in enumerate(rows):
        scale = table_ref[16 + i : 17 + i, :]
        vorticity = (lon_diff(1, i) - lat_diff(0, i)) * scale
        divergence = (lon_diff(0, i) + lat_diff(1, i)) * scale
        x_ref[2 * index] = vorticity
        x_ref[2 * index + 1] = divergence
        largest = jnp.maximum(largest, jnp.maximum(jnp.abs(vorticity), jnp.abs(divergence)))
    bound = jnp.broadcast_to(jnp.max(largest, axis=1, keepdims=True), shape)
    for chunk in range(2 * len(rows)):
        for part, value in enumerate(split_parts(x_ref[chunk], None, bound, X_PARTS)):
            parts_ref[part * SNAPS : (part + 1) * SNAPS, chunk * LANES : (chunk + 1) * LANES] = value
    size = X_PARTS * SNAPS
    high, low = jnp.zeros((size, size), jnp.float32), jnp.zeros((size, size), jnp.float32)
    for index in range(len(rows)):
        piece = parts_ref[:, index * 2 * LANES : (index + 1) * 2 * LANES]
        product = lax.dot_general(
            piece, piece, (((1,), (1,)), ((), ())), preferred_element_type=jnp.float32
        )
        high, error = two_sum(high, product)
        low = low + error
    total = None
    for part in reversed(range(X_PARTS)):
        place = slice(part * SNAPS, (part + 1) * SNAPS)
        pair = (high[place], low[place])
        total = pair if total is None else pair_add(total, pair)
    return fold_parts(total, X_PARTS)


def inner_kernel(u_ref, v_ref, low_lon_ref, high_lon_ref, table_ref, parts_ref, pair_ref, x_ref):
    winds, lon_halos = (u_ref, v_ref), (low_lon_ref, high_lon_ref)
    pair = cut_and_multiply(winds, None, lon_halos, table_ref, INNER, parts_ref, x_ref)
    pair_ref[0], pair_ref[1] = pair


def edge_kernel(
    u_ref, v_ref, low_lat_ref, high_lat_ref, low_lon_ref, high_lon_ref, table_ref, pair_ref, parts_ref, gram_ref, x_ref
):
    winds, lon_halos, lat_halos = (u_ref, v_ref), (low_lon_ref, high_lon_ref), (low_lat_ref, high_lat_ref)
    pair = cut_and_multiply(winds, lat_halos, lon_halos, table_ref, EDGES, parts_ref, x_ref)
    packed, last = pack_pair(pair_add(pair, (pair_ref[0], pair_ref[1])))
    store_copies(gram_ref, [packed[r : r + 1, :] for r in range(8)] + [last])


def store_copies(ref, rows):
    copies = ref.shape[0] // PACKED
    for r, row in enumerate(rows):
        ref[pl.ds(r, copies, stride=PACKED), :] = jnp.broadcast_to(row[0:1, :], (copies, LANES))


def group_lane(shape):
    return lane_iota(shape) % 32


def pack_pair(pair):
    shape = (8, LANES)
    row, group = row_iota(shape), group_lane(shape)
    packed = None
    for b in range(4):
        merged = []
        for value, offset in zip(pair, (0, 16)):
            block = value[8 * b : 8 * b + 8]
            base = (8 * b - offset) % 32
            near = pltpu.roll(block, LANES - base, 1) if base else block
            block = jnp.where(row % 2 == 1, pltpu.roll(block, LANES - base - 1, 1), near)
            block = jnp.where(row % 4 >= 2, pltpu.roll(block, LANES - 2, 1), block)
            block = jnp.where(row >= 4, pltpu.roll(block, LANES - 4, 1), block)
            merged.append(block)
        block = jnp.where(group < 16, merged[0], merged[1])
        packed = block if packed is None else jnp.where(lane_iota(shape) < 32 * b, packed, block)
    half = (16, LANES)
    row, group = row_iota(half), group_lane(half)
    high = jnp.where(group == row, pltpu.roll(pair[0][:16], 16, 1), 0.0)
    low = jnp.where(group == row + 16, pair[1][:16], 0.0)
    return packed, jnp.sum(high + low, axis=0, keepdims=True)


def unpack_pair(rows):
    shape = (8, LANES)
    packed = rows[0]
    for r in range(1, 8):
        packed = jnp.where(row_iota(shape) == r, rows[r], packed)
    full = (SNAPS, LANES)
    row, lane = row_iota(full), lane_iota(full)
    distance = (lane - row) % 32
    last = jnp.concatenate([rows[8]] * 4, axis=0)
    result = []
    for offset in (0, 16):
        blocks = []
        for g in range(4):
            block = jnp.where(lane_iota(shape) < 16, pltpu.roll(packed, (-32 * g - offset) % LANES, 1), 0.0)
            blocks.append(pltpu.roll(block, 8 * g, 1, stride=1, stride_axis=0))
        right = jnp.concatenate(blocks, axis=0)
        right = jnp.where(lane < 32, right + pltpu.roll(right, LANES - 32, 1), 0.0)
        if offset:
            sides = jnp.where(row < 16, last, pltpu.roll(last, LANES - 16, 1))
        else:
            sides = jnp.where(row < 16, pltpu.roll(last, 16, 1), last)
        mirrored = jnp.concatenate([right, jnp.zeros((LANES - SNAPS, LANES), jnp.float32)], axis=0).T[:SNAPS]
        value = jnp.where(distance < 16, right, jnp.where(distance == 16, sides, mirrored))
        result.append(jnp.where(lane < 32, value, 0.0))
    return result


def add_pairs(ref):
    count = ref.shape[0] // PACKED
    group = group_lane((8, LANES))
    rows = []
    for r in range(PACKED):
        values = ref[pl.ds(r, count, stride=PACKED), :]
        if count % 8:
            values = jnp.concatenate([values, jnp.zeros((-count % 8, LANES), jnp.float32)], axis=0)
        terms = [(values[k : k + 8], None) for k in range(0, values.shape[0], 8)]
        while len(terms) > 1:
            terms = [add_terms(a, b) for a, b in zip(terms[::2], terms[1::2])]
        total = terms[0]
        for shift in (4, 2, 1):
            other = tuple(None if x is None else pltpu.roll(x, shift, 0) for x in total)
            total = add_terms(total, other)
        low = pltpu.roll(total[0], LANES - 16, 1) + total[1]
        high = total[0] + low
        low = low - (high - total[0])
        rows.append(jnp.where(group < 16, high, pltpu.roll(low, 16, 1)))
    return rows


def add_terms(a, b):
    total, error = two_sum(a[0], b[0])
    for known in (a[1], b[1]):
        if known is not None:
            error = error + known
    return total, error


def merge_kernel(all_ref, out_ref):
    store_copies(out_ref, add_pairs(all_ref))


def factor_and_inverse(square):
    shape = (8, LANES)
    lane, row = lane_iota(shape), row_iota(shape)
    blocks = [
        jnp.where(lane == row + (32 + 8 * b), 1.0, square[8 * b : 8 * b + 8]) for b in range(4)
    ]
    pivots = [jnp.ones(shape, jnp.float32) for _ in range(4)]

    def spread_lane(value, k):
        return jnp.broadcast_to(value[:, k : k + 1], shape)

    def spread_row(value, k):
        return jnp.broadcast_to(value[k : k + 1, :], shape)

    for k in range(0, SNAPS, 2):
        b, j = divmod(k, 8)
        first = [spread_lane(block, k) for block in blocks[b:]]
        second = [spread_lane(block, k + 1) for block in blocks[b:]]
        row0 = spread_row(blocks[b], j)
        row1 = spread_row(blocks[b], j + 1)
        pivot0 = spread_row(first[0], j)
        below = spread_row(first[0], j + 1)
        beside = spread_row(second[0], j)
        corner = spread_row(second[0], j + 1)
        inverse0 = 1.0 / pivot0
        ratio = below * inverse0
        row1 = row1 - ratio * row0
        pivot1 = corner - ratio * beside
        inverse1 = 1.0 / pivot1
        for index in range(b, 4):
            left = first[index - b] * inverse0
            right = (second[index - b] - left * beside) * inverse1
            new = blocks[index] - left * row0 - right * row1
            if index == b:
                new = jnp.where(row > j + 1, new, blocks[b])
                new = jnp.where(row == j + 1, row1, new)
            blocks[index] = new
        pivots[b] = jnp.where(row == j, pivot0, jnp.where(row == j + 1, pivot1, pivots[b]))
    upper, lower = [], []
    for b in range(4):
        scale = lax.rsqrt(pivots[b])
        scale = scale * (1.5 - 0.5 * pivots[b] * scale * scale)
        scaled = blocks[b] * scale
        upper.append(jnp.where(jnp.logical_and(lane >= row + 8 * b, lane < 32), scaled, 0.0))
        lower.append(jnp.where(lane < 32, pltpu.roll(scaled, LANES - 32, 1), 0.0))
    return jnp.concatenate(upper, axis=0), jnp.concatenate(lower, axis=0)


def product_of_parts(left, right):
    count = len(right)
    tiles = -(-count // 4)
    rows = jnp.concatenate(left, axis=0)
    columns = jnp.concatenate(list(right) + [jnp.zeros_like(right[0])] * (4 * tiles - count), axis=0)
    blocks = lax.dot_general(
        rows, columns, (((1,), (1,)), ((), ())), preferred_element_type=jnp.float32
    )
    total = None
    for part in reversed(range(len(left))):
        value = blocks[part * SNAPS : (part + 1) * SNAPS, :]
        pair = (value, jnp.zeros_like(value))
        total = pair if total is None else pair_add(total, pair)
    lane = lane_iota((SNAPS, LANES))
    return tuple(jnp.where(lane < 32, value, 0.0) for value in fold_parts(total, count))


def row_bound(value):
    return jnp.broadcast_to(jnp.max(jnp.abs(value), axis=1, keepdims=True), value.shape)


def exact_dot(left, right, contract):
    return lax.dot_general(
        left,
        right,
        (contract, ((), ())),
        precision=lax.Precision.HIGHEST,
        preferred_element_type=jnp.float32,
    )


def modes_kernel(root, all_ref, inner_ref, edge_ref, modes_ref, factor_ref):
    high, low = unpack_pair(add_pairs(all_ref))
    first, first_inverse = factor_and_inverse(high)
    gram_parts = [p[:, :32] for p in split_parts(high, low, row_bound(high), G_PARTS)]
    inverse_parts = [p[:, :32] for p in split_parts(first_inverse, None, row_bound(first_inverse), X_PARTS)]
    half = product_of_parts(inverse_parts, gram_parts)
    half_parts = [p[:, :32] for p in split_parts(half[0], half[1], row_bound(half[0]), G_PARTS)]
    second_gram = product_of_parts(half_parts, inverse_parts)[0]
    second, second_inverse = factor_and_inverse(second_gram)
    factor_ref[...] = exact_dot(second[:, :32], first[:, :32], ((1,), (0,))) * (1.0 / root)
    weights = exact_dot(second_inverse[:, :32], first_inverse[:, :32], ((1,), (0,))) * root
    weights = jnp.concatenate([weights] * 4, axis=1)
    pieces = []
    for _ in range(3):
        piece = weights.astype(jnp.bfloat16)
        pieces.append(piece)
        weights = weights - piece.astype(jnp.float32)
    stacked = jnp.concatenate(pieces, axis=0)
    for rows, parts_ref in ((INNER, inner_ref), (EDGES, edge_ref)):
        for index, i in enumerate(rows):
            product = jnp.dot(
                stacked,
                parts_ref[:, index * 2 * LANES : (index + 1) * 2 * LANES],
                preferred_element_type=jnp.float32,
            )
            value = (product[64:96] + product[32:64]) + product[0:32]
            for field in range(2):
                place = pl.ds(field * ROWS + i, SNAPS, stride=CHUNKS)
                modes_ref[place, :] = value[:, field * LANES : (field + 1) * LANES]


def on_chip(count):
    return [pl.BlockSpec(memory_space=pltpu.VMEM)] * count


def call(kernel, shapes, operands, scratch=(), flops=10**8):
    return pl.pallas_call(
        kernel,
        out_shape=shapes,
        in_specs=on_chip(len(operands)),
        out_specs=on_chip(len(shapes)),
        scratch_shapes=list(scratch),
        compiler_params=pltpu.CompilerParams(vmem_limit_bytes=8 * 2**20),
        cost_estimate=pl.CostEstimate(flops=flops, bytes_accessed=2**19, transcendentals=0),
    )(*operands)


def shards(wind_u, wind_v):
    f32 = functools.partial(jax.ShapeDtypeStruct, dtype=jnp.float32)
    bf16 = functools.partial(jax.ShapeDtypeStruct, dtype=jnp.bfloat16)
    lat_axis, lon_axis = "lat", ("z", "core")
    lat_count, lon_count = lax.axis_size(lat_axis), lax.axis_size(lon_axis)
    near, far = lax.axis_size((lat_axis, "core")), lax.axis_size("z")
    u = wind_u.reshape(SNAPS * ROWS, LANES)
    v = wind_v.reshape(SNAPS * ROWS, LANES)

    with jax.named_scope("halo"):
        up = [(i, i + 1) for i in range(lat_count - 1)]
        around = [(i, (i + 1) % lon_count) for i in range(lon_count)]
        back = lambda pairs: [(target, source) for source, target in pairs]
        north, south = call(rows_kernel, [f32((2 * SNAPS, LANES))] * 2, (u, v))
        low_lat = lax.ppermute(south, lat_axis, up)
        high_lat = lax.ppermute(north, lat_axis, back(up))
        west, east = call(sides_kernel, [f32((1, CHUNKS * SNAPS))] * 2, (u, v), flops=10**9)
        low_lon = lax.ppermute(east, lon_axis, around)
        high_lon = lax.ppermute(west, lon_axis, back(around))

    with jax.named_scope("table"):
        step = 2.0 * math.pi / (lon_count * LANES)
        line = row_iota((24, LANES))
        first_row = lax.axis_index(lat_axis) * ROWS
        index = (first_row + jnp.where(line < 16, line - 1, line - 16)).astype(jnp.float32)
        cosine = jnp.cos((index + 0.5 - lat_count * ROWS / 2) * step)
        table = jnp.where(line < 16, cosine, 0.5 / jnp.sqrt(cosine))

    with jax.named_scope("gram"):
        height, width = X_PARTS * SNAPS, 2 * LANES
        inner_parts, pair = call(
            inner_kernel,
            [bf16((height, len(INNER) * width)), f32((2, SNAPS, LANES))],
            (u, v, low_lon, high_lon, table),
            [pltpu.VMEM((2 * len(INNER), SNAPS, LANES), jnp.float32)],
            flops=2 * 10**9,
        )
        edge_parts, gram = call(
            edge_kernel,
            [bf16((height, len(EDGES) * width)), f32((near * PACKED, LANES))],
            (u, v, low_lat, high_lat, low_lon, high_lon, table, pair),
            [pltpu.VMEM((2 * len(EDGES), SNAPS, LANES), jnp.float32)],
        )

    def exchange(copies, axis):
        flat = copies.reshape(-1, 1, PACKED * LANES)
        return lax.all_to_all(flat, axis, 0, 0, tiled=True).reshape(copies.shape)

    with jax.named_scope("sum_near"):
        gathered = exchange(gram, (lat_axis, "core"))
        (gram,) = call(merge_kernel, [f32((far * PACKED, LANES))], (gathered,))
    with jax.named_scope("sum_far"):
        gathered = exchange(gram, "z")

    with jax.named_scope("modes"):
        root = math.sqrt(lat_count * lon_count * CHUNKS * LANES)
        modes, factor = call(
            functools.partial(modes_kernel, root),
            [f32((SNAPS * CHUNKS, LANES)), f32((SNAPS, SNAPS))],
            (gathered, inner_parts, edge_parts),
        )
    return modes.reshape(SNAPS, 2, ROWS, LANES), factor


def solution(mesh):
    lat_count, lon_count = mesh.devices.shape
    inner = Mesh(mesh.devices.reshape(lat_count, lon_count // 2, 2), ("lat", "z", "core"))
    spec = P(None, "lat", ("z", "core"))
    return jax.shard_map(
        shards,
        mesh=inner,
        in_specs=(spec, spec),
        out_specs=(P(None, None, "lat", ("z", "core")), P()),
        check_vma=False,
    )
```

```python
import functools
import math

import jax
import jax.numpy as jnp
from jax import lax
from jax.experimental import pallas as pl
from jax.experimental.pallas import tpu as pltpu
from jax.sharding import Mesh, PartitionSpec as P

SNAPS = 32
ROWS = 8
LANES = 128
CHUNKS = 2 * ROWS
X_PARTS = 4
G_PARTS = 5
PACKED = 9
EDGES = (0, ROWS - 1)
INNER = tuple(range(1, ROWS - 1))


def two_sum(a, b):
    total = a + b
    part = total - a
    return total, (a - (total - part)) + (b - part)


def pair_add(a, b):
    total, error = two_sum(a[0], b[0])
    error = error + (a[1] + b[1])
    high = total + error
    return high, error - (high - total)


def split_parts(value, low, bound, count):
    parts = []
    grid = bound * 2.0**17
    for index in range(count):
        part = (value + grid) - grid
        parts.append(part.astype(jnp.bfloat16))
        value = value - part
        if low is not None and index == 2:
            value = value + low
        grid = grid * 2.0**-8
    return parts


def lane_iota(shape):
    return lax.broadcasted_iota(jnp.int32, shape, 1)


def row_iota(shape):
    return lax.broadcasted_iota(jnp.int32, shape, 0)


def edge_picker():
    shape = (8, LANES)
    row, lane = row_iota(shape), lane_iota(shape)
    first = jnp.logical_and(row == 0, lane == 0)
    last = jnp.logical_and(row == 1, lane == LANES - 1)
    return jnp.where(jnp.logical_or(first, last), 1.0, 0.0).astype(jnp.float32)


def tile_row(ref, field, index):
    return ref[pl.ds(field * SNAPS * ROWS + index, SNAPS, stride=ROWS), :]


def rows_kernel(winds_ref, north_ref, south_ref):
    for field in range(2):
        place = slice(field * SNAPS, (field + 1) * SNAPS)
        north_ref[place, :] = tile_row(winds_ref, field, 0)
        south_ref[place, :] = tile_row(winds_ref, field, ROWS - 1)


def sides_kernel(winds_ref, _, west_ref, east_ref):
    rows = [tile_row(winds_ref, field, i) for i in range(ROWS) for field in range(2)]
    sides = exact_dot(edge_picker(), jnp.concatenate(rows, axis=0), ((1,), (1,)))
    west_ref[...] = sides[0:1, :]
    east_ref[...] = sides[1:2, :]


def fold_parts(blocks, count):
    total = None
    for part in reversed(range(count)):
        tile, group = divmod(part, 4)
        pair = tuple(block[:, tile * LANES : (tile + 1) * LANES] for block in blocks)
        if group:
            pair = tuple(pltpu.roll(block, LANES - 32 * group, 1) for block in pair)
        total = pair if total is None else pair_add(total, pair)
    return total


def cut_and_multiply(winds_ref, lat_halos, lon_halos, table_ref, rows, parts_ref, x_ref):
    shape = (SNAPS, LANES)
    lane = lane_iota(shape)
    low, high = lon_halos[0][...], lon_halos[1][...]
    if rows == EDGES:
        left = lane_iota((1, LANES)) < LANES // 2
        low, high = (jnp.where(left, side[:, :LANES], side[:, -LANES:]) for side in (low, high))
        starts = {0: 0, ROWS - 1: 2 * SNAPS}
    else:
        starts = {i: 2 * SNAPS * i for i in rows}
    row = row_iota((8, low.shape[1]))
    edges = jnp.where(row == 0, low, jnp.where(row == 1, high, 0.0))
    beyond = exact_dot(edges, edge_picker(), ((0,), (0,)))

    def lon_diff(field, i):
        value = tile_row(winds_ref, field, i)
        start = starts[i] + field * SNAPS
        outer = beyond[start : start + SNAPS, :]
        after = jnp.where(lane == LANES - 1, outer, pltpu.roll(value, LANES - 1, 1))
        before = jnp.where(lane == 0, outer, pltpu.roll(value, 1, 1))
        return after - before

    def weighted(field, i):
        if 0 <= i < ROWS:
            value = tile_row(winds_ref, field, i)
        else:
            value = lat_halos[i >= ROWS][field * SNAPS : (field + 1) * SNAPS, :]
        return table_ref[i + 1 : i + 2, :] * value

    def lat_diff(field, i):
        return weighted(field, i + 1) - weighted(field, i - 1)

    largest = jnp.zeros(shape, jnp.float32)
    for index, i in enumerate(rows):
        scale = table_ref[16 + i : 17 + i, :]
        vorticity = (lon_diff(1, i) - lat_diff(0, i)) * scale
        divergence = (lon_diff(0, i) + lat_diff(1, i)) * scale
        x_ref[2 * index] = vorticity
        x_ref[2 * index + 1] = divergence
        largest = jnp.maximum(largest, jnp.maximum(jnp.abs(vorticity), jnp.abs(divergence)))
    bound = jnp.broadcast_to(jnp.max(largest, axis=1, keepdims=True), shape)
    for chunk in range(2 * len(rows)):
        for part, value in enumerate(split_parts(x_ref[chunk], None, bound, X_PARTS)):
            parts_ref[part * SNAPS : (part + 1) * SNAPS, chunk * LANES : (chunk + 1) * LANES] = value
    size = X_PARTS * SNAPS
    high, low = jnp.zeros((size, size), jnp.float32), jnp.zeros((size, size), jnp.float32)
    for index in range(len(rows)):
        piece = parts_ref[:, index * 2 * LANES : (index + 1) * 2 * LANES]
        product = lax.dot_general(
            piece, piece, (((1,), (1,)), ((), ())), preferred_element_type=jnp.float32
        )
        high, error = two_sum(high, product)
        low = low + error
    total = None
    for part in reversed(range(X_PARTS)):
        place = slice(part * SNAPS, (part + 1) * SNAPS)
        pair = (high[place], low[place])
        total = pair if total is None else pair_add(total, pair)
    return fold_parts(total, X_PARTS)


def inner_kernel(winds_ref, low_lon_ref, high_lon_ref, table_ref, parts_ref, pair_ref, x_ref):
    lon_halos = (low_lon_ref, high_lon_ref)
    pair = cut_and_multiply(winds_ref, None, lon_halos, table_ref, INNER, parts_ref, x_ref)
    pair_ref[0], pair_ref[1] = pair


def edge_kernel(
    winds_ref, low_lat_ref, high_lat_ref, low_lon_ref, high_lon_ref, table_ref, pair_ref, parts_ref, gram_ref, x_ref
):
    lon_halos, lat_halos = (low_lon_ref, high_lon_ref), (low_lat_ref, high_lat_ref)
    pair = cut_and_multiply(winds_ref, lat_halos, lon_halos, table_ref, EDGES, parts_ref, x_ref)
    packed, last = pack_pair(pair_add(pair, (pair_ref[0], pair_ref[1])))
    store_copies(gram_ref, [packed[r : r + 1, :] for r in range(8)] + [last])


def store_copies(ref, rows):
    copies = ref.shape[0] // PACKED
    for r, row in enumerate(rows):
        ref[pl.ds(r, copies, stride=PACKED), :] = jnp.broadcast_to(row[0:1, :], (copies, LANES))


def group_lane(shape):
    return lane_iota(shape) % 32


def pack_pair(pair):
    shape = (8, LANES)
    row, group = row_iota(shape), group_lane(shape)
    packed = None
    for b in range(4):
        merged = []
        for value, offset in zip(pair, (0, 16)):
            block = value[8 * b : 8 * b + 8]
            base = (8 * b - offset) % 32
            near = pltpu.roll(block, LANES - base, 1) if base else block
            block = jnp.where(row % 2 == 1, pltpu.roll(block, LANES - base - 1, 1), near)
            block = jnp.where(row % 4 >= 2, pltpu.roll(block, LANES - 2, 1), block)
            block = jnp.where(row >= 4, pltpu.roll(block, LANES - 4, 1), block)
            merged.append(block)
        block = jnp.where(group < 16, merged[0], merged[1])
        packed = block if packed is None else jnp.where(lane_iota(shape) < 32 * b, packed, block)
    half = (16, LANES)
    row, group = row_iota(half), group_lane(half)
    high = jnp.where(group == row, pltpu.roll(pair[0][:16], 16, 1), 0.0)
    low = jnp.where(group == row + 16, pair[1][:16], 0.0)
    return packed, jnp.sum(high + low, axis=0, keepdims=True)


def unpack_pair(rows):
    shape = (8, LANES)
    packed = rows[0]
    for r in range(1, 8):
        packed = jnp.where(row_iota(shape) == r, rows[r], packed)
    full = (SNAPS, LANES)
    row, lane = row_iota(full), lane_iota(full)
    distance = (lane - row) % 32
    last = jnp.concatenate([rows[8]] * 4, axis=0)
    result = []
    for offset in (0, 16):
        blocks = []
        for g in range(4):
            block = jnp.where(lane_iota(shape) < 16, pltpu.roll(packed, (-32 * g - offset) % LANES, 1), 0.0)
            blocks.append(pltpu.roll(block, 8 * g, 1, stride=1, stride_axis=0))
        right = jnp.concatenate(blocks, axis=0)
        right = jnp.where(lane < 32, right + pltpu.roll(right, LANES - 32, 1), 0.0)
        if offset:
            sides = jnp.where(row < 16, last, pltpu.roll(last, LANES - 16, 1))
        else:
            sides = jnp.where(row < 16, pltpu.roll(last, 16, 1), last)
        mirrored = jnp.concatenate([right, jnp.zeros((LANES - SNAPS, LANES), jnp.float32)], axis=0).T[:SNAPS]
        value = jnp.where(distance < 16, right, jnp.where(distance == 16, sides, mirrored))
        result.append(jnp.where(lane < 32, value, 0.0))
    return result


def add_pairs(ref):
    count = ref.shape[0] // PACKED
    group = group_lane((8, LANES))
    rows = []
    for r in range(PACKED):
        values = ref[pl.ds(r, count, stride=PACKED), :]
        if count % 8:
            values = jnp.concatenate([values, jnp.zeros((-count % 8, LANES), jnp.float32)], axis=0)
        terms = [(values[k : k + 8], None) for k in range(0, values.shape[0], 8)]
        while len(terms) > 1:
            terms = [add_terms(a, b) for a, b in zip(terms[::2], terms[1::2])]
        total = terms[0]
        for shift in (4, 2, 1):
            other = tuple(None if x is None else pltpu.roll(x, shift, 0) for x in total)
            total = add_terms(total, other)
        low = pltpu.roll(total[0], LANES - 16, 1) + total[1]
        high = total[0] + low
        low = low - (high - total[0])
        rows.append(jnp.where(group < 16, high, pltpu.roll(low, 16, 1)))
    return rows


def add_terms(a, b):
    total, error = two_sum(a[0], b[0])
    for known in (a[1], b[1]):
        if known is not None:
            error = error + known
    return total, error


def merge_kernel(all_ref, out_ref):
    store_copies(out_ref, add_pairs(all_ref))


def factor_and_inverse(square):
    shape = (8, LANES)
    lane, row = lane_iota(shape), row_iota(shape)
    blocks = [
        jnp.where(lane == row + (32 + 8 * b), 1.0, square[8 * b : 8 * b + 8]) for b in range(4)
    ]
    upper, lower = [], []
    for b in range(4):
        columns = [
            [jnp.broadcast_to(block[:, 8 * b + w : 8 * b + w + 1], shape) for block in blocks[b:]]
            for w in range(8)
        ]
        rows = [jnp.broadcast_to(blocks[b][w : w + 1, :], shape) for w in range(8)]
        corner = [
            [jnp.broadcast_to(columns[t][0][w : w + 1, :], shape) if t >= w else None for t in range(8)]
            for w in range(8)
        ]
        pivots, done = corner[0][0], rows[0]
        for w in range(8):
            inverse = 1.0 / corner[w][w]
            for t in range(w + 1, 8):
                ratio = corner[w][t] * inverse
                rows[t] = rows[t] - ratio * rows[w]
                for s in range(t, 8):
                    corner[t][s] = corner[t][s] - ratio * corner[w][s]
            for i in range(1, 4 - b):
                left = columns[w][i] * inverse
                for t in range(w + 1, 8):
                    columns[t][i] = columns[t][i] - left * corner[w][t]
                blocks[b + i] = blocks[b + i] - left * rows[w]
            if w:
                pivots = jnp.where(row == w, corner[w][w], pivots)
                done = jnp.where(row == w, rows[w], done)
        scale = lax.rsqrt(pivots)
        scaled = done * (scale * (1.5 - 0.5 * pivots * scale * scale))
        upper.append(jnp.where(jnp.logical_and(lane >= row + 8 * b, lane < 32), scaled, 0.0))
        lower.append(jnp.where(lane < 32, pltpu.roll(scaled, LANES - 32, 1), 0.0))
    return jnp.concatenate(upper, axis=0), jnp.concatenate(lower, axis=0)


def product_of_parts(left, right):
    count = len(right)
    tiles = -(-count // 4)
    rows = jnp.concatenate(left, axis=0)
    columns = jnp.concatenate(list(right) + [jnp.zeros_like(right[0])] * (4 * tiles - count), axis=0)
    blocks = lax.dot_general(
        rows, columns, (((1,), (1,)), ((), ())), preferred_element_type=jnp.float32
    )
    total = None
    for part in reversed(range(len(left))):
        value = blocks[part * SNAPS : (part + 1) * SNAPS, :]
        pair = (value, jnp.zeros_like(value))
        total = pair if total is None else pair_add(total, pair)
    lane = lane_iota((SNAPS, LANES))
    return tuple(jnp.where(lane < 32, value, 0.0) for value in fold_parts(total, count))


def row_bound(value):
    return jnp.broadcast_to(jnp.max(jnp.abs(value), axis=1, keepdims=True), value.shape)


def exact_dot(left, right, contract):
    return lax.dot_general(
        left,
        right,
        (contract, ((), ())),
        precision=lax.Precision.HIGHEST,
        preferred_element_type=jnp.float32,
    )


def modes_kernel(root, all_ref, inner_ref, edge_ref, modes_ref, factor_ref):
    high, low = unpack_pair(add_pairs(all_ref))
    first, first_inverse = factor_and_inverse(high)
    gram_parts = [p[:, :32] for p in split_parts(high, low, row_bound(high), G_PARTS)]
    inverse_parts = [p[:, :32] for p in split_parts(first_inverse, None, row_bound(first_inverse), X_PARTS)]
    half = product_of_parts(inverse_parts, gram_parts)
    half_parts = [p[:, :32] for p in split_parts(half[0], half[1], row_bound(half[0]), G_PARTS)]
    second_gram = product_of_parts(half_parts, inverse_parts)[0]
    second, second_inverse = factor_and_inverse(second_gram)
    factor_ref[...] = exact_dot(second[:, :32], first[:, :32], ((1,), (0,))) * (1.0 / root)
    weights = exact_dot(second_inverse[:, :32], first_inverse[:, :32], ((1,), (0,))) * root
    weights = jnp.concatenate([weights] * 4, axis=1)
    pieces = []
    for _ in range(3):
        piece = weights.astype(jnp.bfloat16)
        pieces.append(piece)
        weights = weights - piece.astype(jnp.float32)
    stacked = jnp.concatenate(pieces, axis=0)
    for rows, parts_ref in ((INNER, inner_ref), (EDGES, edge_ref)):
        for index, i in enumerate(rows):
            product = jnp.dot(
                stacked,
                parts_ref[:, index * 2 * LANES : (index + 1) * 2 * LANES],
                preferred_element_type=jnp.float32,
            )
            value = (product[64:96] + product[32:64]) + product[0:32]
            for field in range(2):
                place = pl.ds(field * ROWS + i, SNAPS, stride=CHUNKS)
                modes_ref[place, :] = value[:, field * LANES : (field + 1) * LANES]


def call(kernel, shapes, operands, scratch=(), flops=10**8):
    return pl.pallas_call(
        kernel,
        out_shape=shapes,
        in_specs=[pl.BlockSpec(memory_space=pltpu.VMEM)] * len(operands),
        out_specs=[pl.BlockSpec(memory_space=pltpu.VMEM)] * len(shapes),
        scratch_shapes=list(scratch),
        compiler_params=pltpu.CompilerParams(vmem_limit_bytes=8 * 2**20),
        cost_estimate=pl.CostEstimate(flops=flops, bytes_accessed=2**19, transcendentals=0),
    )(*operands)


def shards(wind_u, wind_v):
    f32 = functools.partial(jax.ShapeDtypeStruct, dtype=jnp.float32)
    bf16 = functools.partial(jax.ShapeDtypeStruct, dtype=jnp.bfloat16)
    lat_axis, lon_axis = "lat", ("z", "core")
    lat_count, lon_count = lax.axis_size(lat_axis), lax.axis_size(lon_axis)
    near, far = lax.axis_size((lat_axis, "core")), lax.axis_size("z")
    winds = jnp.stack([wind_u, wind_v]).reshape(2 * SNAPS * ROWS, LANES)

    with jax.named_scope("halo"):
        up = [(i, i + 1) for i in range(lat_count - 1)]
        around = [(i, (i + 1) % lon_count) for i in range(lon_count)]
        back = lambda pairs: [(target, source) for source, target in pairs]
        north, south = call(rows_kernel, [f32((2 * SNAPS, LANES))] * 2, (winds,))
        low_lat = lax.ppermute(south, lat_axis, up)
        high_lat = lax.ppermute(north, lat_axis, back(up))
        west, east = call(sides_kernel, [f32((1, CHUNKS * SNAPS))] * 2, (winds, low_lat), flops=10**9)
        low_lon = lax.ppermute(east, lon_axis, around)
        high_lon = lax.ppermute(west, lon_axis, back(around))

    with jax.named_scope("table"):
        step = 2.0 * math.pi / (lon_count * LANES)
        line = row_iota((24, LANES))
        first_row = lax.axis_index(lat_axis) * ROWS
        index = (first_row + jnp.where(line < 16, line - 1, line - 16)).astype(jnp.float32)
        cosine = jnp.cos((index + 0.5 - lat_count * ROWS / 2) * step)
        table = jnp.where(line < 16, cosine, 0.5 / jnp.sqrt(cosine))

    with jax.named_scope("gram"):
        height, width = X_PARTS * SNAPS, 2 * LANES
        inner_parts, pair = call(
            inner_kernel,
            [bf16((height, len(INNER) * width)), f32((2, SNAPS, LANES))],
            (winds, low_lon, high_lon, table),
            [pltpu.VMEM((2 * len(INNER), SNAPS, LANES), jnp.float32)],
            flops=2 * 10**9,
        )
        edge_parts, gram = call(
            edge_kernel,
            [bf16((height, len(EDGES) * width)), f32((near * PACKED, LANES))],
            (winds, low_lat, high_lat, low_lon, high_lon, table, pair),
            [pltpu.VMEM((2 * len(EDGES), SNAPS, LANES), jnp.float32)],
        )

    def exchange(copies, axis):
        flat = copies.reshape(-1, 1, PACKED * LANES)
        return lax.all_to_all(flat, axis, 0, 0, tiled=True).reshape(copies.shape)

    with jax.named_scope("sum_near"):
        gathered = exchange(gram, (lat_axis, "core"))
        (gram,) = call(merge_kernel, [f32((far * PACKED, LANES))], (gathered,))
    with jax.named_scope("sum_far"):
        gathered = exchange(gram, "z")

    with jax.named_scope("modes"):
        root = math.sqrt(lat_count * lon_count * CHUNKS * LANES)
        modes, factor = call(
            functools.partial(modes_kernel, root),
            [f32((SNAPS * CHUNKS, LANES)), f32((SNAPS, SNAPS))],
            (gathered, inner_parts, edge_parts),
        )
    return modes.reshape(SNAPS, 2, ROWS, LANES), factor


def solution(mesh):
    lat_count, lon_count = mesh.devices.shape
    inner = Mesh(mesh.devices.reshape(lat_count, lon_count // 2, 2), ("lat", "z", "core"))
    spec = P(None, "lat", ("z", "core"))
    return jax.shard_map(
        shards,
        mesh=inner,
        in_specs=(spec, spec),
        out_specs=(P(None, None, "lat", ("z", "core")), P()),
        check_vma=False,
    )
```

```python
import functools
import math

import jax
import jax.numpy as jnp
from jax import lax
from jax.experimental import pallas as pl
from jax.experimental.pallas import tpu as pltpu
from jax.sharding import Mesh, PartitionSpec as P

SNAPS = 32
ROWS = 8
LANES = 128
CHUNKS = 2 * ROWS
X_PARTS = 4
G_PARTS = 5
PACKED = 9


def two_sum(a, b):
    total = a + b
    part = total - a
    return total, (a - (total - part)) + (b - part)


def pair_add(a, b):
    total, error = two_sum(a[0], b[0])
    error = error + (a[1] + b[1])
    high = total + error
    return high, error - (high - total)


def split_parts(value, low, bound, count):
    parts = []
    grid = bound * 2.0**17
    for index in range(count):
        part = (value + grid) - grid
        parts.append(part.astype(jnp.bfloat16))
        value = value - part
        if low is not None and index == 2:
            value = value + low
        grid = grid * 2.0**-8
    return parts


def lane_iota(shape):
    return lax.broadcasted_iota(jnp.int32, shape, 1)


def row_iota(shape):
    return lax.broadcasted_iota(jnp.int32, shape, 0)


def tile_row(ref, field, index):
    return ref[pl.ds(field * SNAPS * ROWS + index, SNAPS, stride=ROWS), :]


def rows_kernel(winds_ref, north_ref, south_ref):
    for field in range(2):
        place = slice(field * SNAPS, (field + 1) * SNAPS)
        north_ref[place, :] = tile_row(winds_ref, field, 0)
        south_ref[place, :] = tile_row(winds_ref, field, ROWS - 1)


def side_lanes(lane, chunk):
    return jnp.logical_or(lane == 2 * chunk, lane == (2 * chunk - 1) % LANES)


def gather_sides(values):
    lane = lane_iota((SNAPS, LANES))
    sides = jnp.zeros((SNAPS, LANES), jnp.float32)
    for chunk, value in enumerate(values):
        sides = jnp.where(side_lanes(lane, chunk), turn(value, 2 * chunk), sides)
    return sides


def turn(value, shift):
    return pltpu.roll(value, shift % LANES, 1) if shift % LANES else value


def sides_kernel(winds_ref, _, sides_ref):
    sides_ref[...] = gather_sides(
        [tile_row(winds_ref, 1 - chunk % 2, chunk // 2) for chunk in range(CHUNKS)]
    )


def fold_parts(blocks, count):
    total = None
    for part in reversed(range(count)):
        tile, group = divmod(part, 4)
        pair = tuple(block[:, tile * LANES : (tile + 1) * LANES] for block in blocks)
        if group:
            pair = tuple(pltpu.roll(block, LANES - 32 * group, 1) for block in pair)
        total = pair if total is None else pair_add(total, pair)
    return total


def row_bound(value):
    return jnp.broadcast_to(jnp.max(jnp.abs(value), axis=1, keepdims=True), value.shape)


def cut(value, bound, parts_ref, chunk):
    for part, piece in enumerate(split_parts(value, None, bound, X_PARTS)):
        parts_ref[part * SNAPS : (part + 1) * SNAPS, chunk * LANES : (chunk + 1) * LANES] = piece


def gram_of_parts(parts_ref):
    high = low = None
    for start in range(0, parts_ref.shape[1], 2 * LANES):
        piece = parts_ref[:, start : start + 2 * LANES]
        product = lax.dot_general(
            piece, piece, (((1,), (1,)), ((), ())), preferred_element_type=jnp.float32
        )
        if high is None:
            high, low = product, jnp.zeros_like(product)
        else:
            high, error = two_sum(high, product)
            low = low + error
    total = None
    for part in reversed(range(X_PARTS)):
        place = slice(part * SNAPS, (part + 1) * SNAPS)
        pair = (high[place], low[place])
        total = pair if total is None else pair_add(total, pair)
    return fold_parts(total, X_PARTS)


def inner_kernel(winds_ref, low_lat_ref, high_lat_ref, table_ref, parts_ref, pair_ref, sides_ref, x_ref):
    lane = lane_iota((SNAPS, LANES))

    def lon_diff(field, i):
        value = tile_row(winds_ref, field, i)
        after = jnp.where(lane == LANES - 1, 0.0, turn(value, -1))
        return after - jnp.where(lane == 0, 0.0, turn(value, 1))

    def weighted(field, i):
        if 0 <= i < ROWS:
            value = tile_row(winds_ref, field, i)
        else:
            value = (low_lat_ref if i < 0 else high_lat_ref)[field * SNAPS : (field + 1) * SNAPS, :]
        return table_ref[i + 1 : i + 2, :] * value

    def lat_diff(field, i):
        return weighted(field, i + 1) - weighted(field, i - 1)

    largest = jnp.zeros((SNAPS, LANES), jnp.float32)
    sides = jnp.zeros((SNAPS, LANES), jnp.float32)
    inside = jnp.logical_and(lane > 0, lane < LANES - 1)
    for i in range(ROWS):
        scale = table_ref[16 + i : 17 + i, :]
        vorticity = (lon_diff(1, i) - lat_diff(0, i)) * scale
        divergence = (lon_diff(0, i) + lat_diff(1, i)) * scale
        for chunk, value in ((2 * i, vorticity), (2 * i + 1, divergence)):
            sides = jnp.where(side_lanes(lane, chunk), turn(value, 2 * chunk), sides)
            value = jnp.where(inside, value, 0.0)
            x_ref[chunk] = value
            largest = jnp.maximum(largest, jnp.abs(value))
    sides_ref[...] = sides
    bound = row_bound(largest)
    for chunk in range(CHUNKS):
        cut(x_ref[chunk], bound, parts_ref, chunk)
    pair_ref[0], pair_ref[1] = gram_of_parts(parts_ref)


def edge_kernel(low_lon_ref, high_lon_ref, table_ref, pair_ref, sides_ref, parts_ref, gram_ref):
    lane = lane_iota((SNAPS, LANES))
    before, after = turn(low_lon_ref[...], 1), turn(high_lon_ref[...], -1)
    value = sides_ref[...] + jnp.where(lane % 2 == 0, -before, after) * table_ref[24:25, :]
    cut(value, row_bound(value), parts_ref, 0)
    packed, last = pack_pair(pair_add(gram_of_parts(parts_ref), (pair_ref[0], pair_ref[1])))
    store_copies(gram_ref, [packed[r : r + 1, :] for r in range(8)] + [last])


def store_copies(ref, rows):
    copies = ref.shape[0] // PACKED
    for r, row in enumerate(rows):
        ref[pl.ds(r, copies, stride=PACKED), :] = jnp.broadcast_to(row[0:1, :], (copies, LANES))


def group_lane(shape):
    return lane_iota(shape) % 32


def pack_pair(pair):
    shape = (8, LANES)
    row, group = row_iota(shape), group_lane(shape)
    packed = None
    for b in range(4):
        merged = []
        for value, offset in zip(pair, (0, 16)):
            block = value[8 * b : 8 * b + 8]
            base = (8 * b - offset) % 32
            near = pltpu.roll(block, LANES - base, 1) if base else block
            block = jnp.where(row % 2 == 1, pltpu.roll(block, LANES - base - 1, 1), near)
            block = jnp.where(row % 4 >= 2, pltpu.roll(block, LANES - 2, 1), block)
            block = jnp.where(row >= 4, pltpu.roll(block, LANES - 4, 1), block)
            merged.append(block)
        block = jnp.where(group < 16, merged[0], merged[1])
        packed = block if packed is None else jnp.where(lane_iota(shape) < 32 * b, packed, block)
    half = (16, LANES)
    row, group = row_iota(half), group_lane(half)
    high = jnp.where(group == row, pltpu.roll(pair[0][:16], 16, 1), 0.0)
    low = jnp.where(group == row + 16, pair[1][:16], 0.0)
    return packed, jnp.sum(high + low, axis=0, keepdims=True)


def unpack_pair(rows):
    shape = (8, LANES)
    packed = rows[0]
    for r in range(1, 8):
        packed = jnp.where(row_iota(shape) == r, rows[r], packed)
    full = (SNAPS, LANES)
    row, lane = row_iota(full), lane_iota(full)
    distance = (lane - row) % 32
    last = jnp.concatenate([rows[8]] * 4, axis=0)
    result = []
    for offset in (0, 16):
        blocks = []
        for g in range(4):
            block = jnp.where(lane_iota(shape) < 16, pltpu.roll(packed, (-32 * g - offset) % LANES, 1), 0.0)
            blocks.append(pltpu.roll(block, 8 * g, 1, stride=1, stride_axis=0))
        right = jnp.concatenate(blocks, axis=0)
        right = jnp.where(lane < 32, right + pltpu.roll(right, LANES - 32, 1), 0.0)
        if offset:
            sides = jnp.where(row < 16, last, pltpu.roll(last, LANES - 16, 1))
        else:
            sides = jnp.where(row < 16, pltpu.roll(last, 16, 1), last)
        mirrored = jnp.concatenate([right, jnp.zeros((LANES - SNAPS, LANES), jnp.float32)], axis=0).T[:SNAPS]
        value = jnp.where(distance < 16, right, jnp.where(distance == 16, sides, mirrored))
        result.append(jnp.where(lane < 32, value, 0.0))
    return result


def add_pairs(ref):
    count = ref.shape[0] // PACKED
    group = group_lane((8, LANES))
    rows = []
    for r in range(PACKED):
        values = ref[pl.ds(r, count, stride=PACKED), :]
        if count % 8:
            values = jnp.concatenate([values, jnp.zeros((-count % 8, LANES), jnp.float32)], axis=0)
        terms = [(values[k : k + 8], None) for k in range(0, values.shape[0], 8)]
        while len(terms) > 1:
            terms = [add_terms(a, b) for a, b in zip(terms[::2], terms[1::2])]
        total = terms[0]
        for shift in (4, 2, 1):
            other = tuple(None if x is None else pltpu.roll(x, shift, 0) for x in total)
            total = add_terms(total, other)
        low = pltpu.roll(total[0], LANES - 16, 1) + total[1]
        high = total[0] + low
        low = low - (high - total[0])
        rows.append(jnp.where(group < 16, high, pltpu.roll(low, 16, 1)))
    return rows


def add_terms(a, b):
    total, error = two_sum(a[0], b[0])
    for known in (a[1], b[1]):
        if known is not None:
            error = error + known
    return total, error


def merge_kernel(all_ref, out_ref):
    store_copies(out_ref, add_pairs(all_ref))


def factor_and_inverse(square):
    shape = (8, LANES)
    lane, row = lane_iota(shape), row_iota(shape)
    blocks = [
        jnp.where(lane == row + (32 + 8 * b), 1.0, square[8 * b : 8 * b + 8]) for b in range(4)
    ]
    upper, lower = [], []
    for b in range(4):
        columns = [
            [jnp.broadcast_to(block[:, 8 * b + w : 8 * b + w + 1], shape) for block in blocks[b:]]
            for w in range(8)
        ]
        rows = [jnp.broadcast_to(blocks[b][w : w + 1, :], shape) for w in range(8)]
        corner = [
            [jnp.broadcast_to(columns[t][0][w : w + 1, :], shape) if t >= w else None for t in range(8)]
            for w in range(8)
        ]
        pivots, done = corner[0][0], rows[0]
        for w in range(8):
            inverse = 1.0 / corner[w][w]
            for t in range(w + 1, 8):
                ratio = corner[w][t] * inverse
                rows[t] = rows[t] - ratio * rows[w]
                for s in range(t, 8):
                    corner[t][s] = corner[t][s] - ratio * corner[w][s]
            for i in range(1, 4 - b):
                left = columns[w][i] * inverse
                for t in range(w + 1, 8):
                    columns[t][i] = columns[t][i] - left * corner[w][t]
                blocks[b + i] = blocks[b + i] - left * rows[w]
            if w:
                pivots = jnp.where(row == w, corner[w][w], pivots)
                done = jnp.where(row == w, rows[w], done)
        scale = lax.rsqrt(pivots)
        scaled = done * (scale * (1.5 - 0.5 * pivots * scale * scale))
        upper.append(jnp.where(jnp.logical_and(lane >= row + 8 * b, lane < 32), scaled, 0.0))
        lower.append(jnp.where(lane < 32, pltpu.roll(scaled, LANES - 32, 1), 0.0))
    return jnp.concatenate(upper, axis=0), jnp.concatenate(lower, axis=0)


def product_of_parts(left, right):
    count = len(right)
    tiles = -(-count // 4)
    rows = jnp.concatenate(left, axis=0)
    columns = jnp.concatenate(list(right) + [jnp.zeros_like(right[0])] * (4 * tiles - count), axis=0)
    blocks = lax.dot_general(
        rows, columns, (((1,), (1,)), ((), ())), preferred_element_type=jnp.float32
    )
    total = None
    for part in reversed(range(len(left))):
        value = blocks[part * SNAPS : (part + 1) * SNAPS, :]
        pair = (value, jnp.zeros_like(value))
        total = pair if total is None else pair_add(total, pair)
    lane = lane_iota((SNAPS, LANES))
    return tuple(jnp.where(lane < 32, value, 0.0) for value in fold_parts(total, count))


def exact_dot(left, right, contract):
    return lax.dot_general(
        left,
        right,
        (contract, ((), ())),
        precision=lax.Precision.HIGHEST,
        preferred_element_type=jnp.float32,
    )


def modes_kernel(root, all_ref, inner_ref, edge_ref, modes_ref, factor_ref):
    lane = lane_iota((SNAPS, LANES))
    high, low = unpack_pair(add_pairs(all_ref))
    first, first_inverse = factor_and_inverse(high)
    gram_parts = [p[:, :32] for p in split_parts(high, low, row_bound(high), G_PARTS)]
    inverse_parts = [p[:, :32] for p in split_parts(first_inverse, None, row_bound(first_inverse), X_PARTS)]
    half = product_of_parts(inverse_parts, gram_parts)
    half_parts = [p[:, :32] for p in split_parts(half[0], half[1], row_bound(half[0]), G_PARTS)]
    second_gram = product_of_parts(half_parts, inverse_parts)[0]
    second, second_inverse = factor_and_inverse(second_gram)
    factor_ref[...] = exact_dot(second[:, :32], first[:, :32], ((1,), (0,))) * (1.0 / root)
    weights = exact_dot(second_inverse[:, :32], first_inverse[:, :32], ((1,), (0,))) * root
    weights = jnp.concatenate([weights] * 4, axis=1)
    pieces = []
    for _ in range(3):
        piece = weights.astype(jnp.bfloat16)
        pieces.append(piece)
        weights = weights - piece.astype(jnp.float32)
    stacked = jnp.concatenate(pieces, axis=0)

    def times(parts):
        product = jnp.dot(stacked, parts, preferred_element_type=jnp.float32)
        return (product[64:96] + product[32:64]) + product[0:32]

    sides = times(edge_ref[...])
    for i in range(ROWS):
        value = times(inner_ref[:, i * 2 * LANES : (i + 1) * 2 * LANES])
        for field in range(2):
            chunk = 2 * i + field
            own = value[:, field * LANES : (field + 1) * LANES]
            ends = jnp.logical_or(lane == 0, lane == LANES - 1)
            place = pl.ds(field * ROWS + i, SNAPS, stride=CHUNKS)
            modes_ref[place, :] = jnp.where(ends, turn(sides, -2 * chunk), own)


def call(kernel, shapes, operands, scratch=(), flops=10**8):
    return pl.pallas_call(
        kernel,
        out_shape=shapes,
        in_specs=[pl.BlockSpec(memory_space=pltpu.VMEM)] * len(operands),
        out_specs=[pl.BlockSpec(memory_space=pltpu.VMEM)] * len(shapes),
        scratch_shapes=list(scratch),
        compiler_params=pltpu.CompilerParams(vmem_limit_bytes=8 * 2**20),
        cost_estimate=pl.CostEstimate(flops=flops, bytes_accessed=2**19, transcendentals=0),
    )(*operands)


def shards(wind_u, wind_v):
    f32 = functools.partial(jax.ShapeDtypeStruct, dtype=jnp.float32)
    bf16 = functools.partial(jax.ShapeDtypeStruct, dtype=jnp.bfloat16)
    lat_axis, lon_axis = "lat", ("z", "core")
    lat_count, lon_count = lax.axis_size(lat_axis), lax.axis_size(lon_axis)
    near, far = lax.axis_size((lat_axis, "core")), lax.axis_size("z")
    winds = jnp.stack([wind_u, wind_v]).reshape(2 * SNAPS * ROWS, LANES)

    with jax.named_scope("halo"):
        up = [(i, i + 1) for i in range(lat_count - 1)]
        around = [(i, (i + 1) % lon_count) for i in range(lon_count)]
        back = lambda pairs: [(target, source) for source, target in pairs]
        north, south = call(rows_kernel, [f32((2 * SNAPS, LANES))] * 2, (winds,))
        low_lat = lax.ppermute(south, lat_axis, up)
        high_lat = lax.ppermute(north, lat_axis, back(up))
        (sides,) = call(sides_kernel, [f32((SNAPS, LANES))], (winds, low_lat))
        low_lon = lax.ppermute(sides, lon_axis, around)
        high_lon = lax.ppermute(sides, lon_axis, back(around))

    with jax.named_scope("table"):
        step = 2.0 * math.pi / (lon_count * LANES)
        line, lane = row_iota((32, LANES)), lane_iota((32, LANES))
        first_row = lax.axis_index(lat_axis) * ROWS
        offset = jnp.where(line < 16, line - 1, jnp.where(line < 24, line - 16, (lane + 1) % LANES // 4))
        index = (first_row + offset).astype(jnp.float32)
        cosine = jnp.cos((index + 0.5 - lat_count * ROWS / 2) * step)
        table = jnp.where(line < 16, cosine, 0.5 / jnp.sqrt(cosine))

    with jax.named_scope("gram"):
        height = X_PARTS * SNAPS
        inner_parts, pair, sides = call(
            inner_kernel,
            [bf16((height, CHUNKS * LANES)), f32((2, SNAPS, LANES)), f32((SNAPS, LANES))],
            (winds, low_lat, high_lat, table),
            [pltpu.VMEM((CHUNKS, SNAPS, LANES), jnp.float32)],
            flops=2 * 10**9,
        )
        edge_parts, gram = call(
            edge_kernel,
            [bf16((height, LANES)), f32((near * PACKED, LANES))],
            (low_lon, high_lon, table, pair, sides),
        )

    def exchange(copies, axis):
        flat = copies.reshape(-1, 1, PACKED * LANES)
        return lax.all_to_all(flat, axis, 0, 0, tiled=True).reshape(copies.shape)

    with jax.named_scope("sum_near"):
        gathered = exchange(gram, (lat_axis, "core"))
        (gram,) = call(merge_kernel, [f32((far * PACKED, LANES))], (gathered,))
    with jax.named_scope("sum_far"):
        gathered = exchange(gram, "z")

    with jax.named_scope("modes"):
        root = math.sqrt(lat_count * lon_count * CHUNKS * LANES)
        modes, factor = call(
            functools.partial(modes_kernel, root),
            [f32((SNAPS * CHUNKS, LANES)), f32((SNAPS, SNAPS))],
            (gathered, inner_parts, edge_parts),
        )
    return modes.reshape(SNAPS, 2, ROWS, LANES), factor


def solution(mesh):
    lat_count, lon_count = mesh.devices.shape
    inner = Mesh(mesh.devices.reshape(lat_count, lon_count // 2, 2), ("lat", "z", "core"))
    spec = P(None, "lat", ("z", "core"))
    return jax.shard_map(
        shards,
        mesh=inner,
        in_specs=(spec, spec),
        out_specs=(P(None, None, "lat", ("z", "core")), P()),
        check_vma=False,
    )
```

```python
import functools
import math

import jax
import jax.numpy as jnp
from jax import lax
from jax.experimental import pallas as pl
from jax.experimental.pallas import tpu as pltpu
from jax.sharding import Mesh, PartitionSpec as P

SNAPS = 32
ROWS = 8
LANES = 128
CHUNKS = 2 * ROWS
X_PARTS = 4
G_PARTS = 5
PACKED = 9


def two_sum(a, b):
    total = a + b
    part = total - a
    return total, (a - (total - part)) + (b - part)


def add_terms(a, b):
    total, error = two_sum(a[0], b[0])
    for known in (a[1], b[1]):
        if known is not None:
            error = error + known
    return total, error


def add_all(terms):
    while len(terms) > 1:
        merged = [add_terms(a, b) for a, b in zip(terms[::2], terms[1::2])]
        terms = merged + terms[2 * len(merged) :]
    return terms[0]


def normalized(term):
    high = term[0] + term[1]
    return high, term[1] - (high - term[0])


def split_parts(value, low, bound, count):
    parts = []
    grid = bound * 2.0**17
    for index in range(count):
        part = (value + grid) - grid
        parts.append(part.astype(jnp.bfloat16))
        value = value - part
        if low is not None and index == 2:
            value = value + low
        grid = grid * 2.0**-8
    return parts


def lane_iota(shape):
    return lax.broadcasted_iota(jnp.int32, shape, 1)


def row_iota(shape):
    return lax.broadcasted_iota(jnp.int32, shape, 0)


def tile_row(ref, field, index):
    return ref[pl.ds(field * SNAPS * ROWS + index, SNAPS, stride=ROWS), :]


def rows_kernel(winds_ref, north_ref, south_ref):
    for field in range(2):
        place = slice(field * SNAPS, (field + 1) * SNAPS)
        north_ref[place, :] = tile_row(winds_ref, field, 0)
        south_ref[place, :] = tile_row(winds_ref, field, ROWS - 1)


def side_lanes(lane, chunk):
    return jnp.logical_or(lane == 2 * chunk, lane == (2 * chunk - 1) % LANES)


def gather_sides(values):
    lane = lane_iota((SNAPS, LANES))
    sides = jnp.zeros((SNAPS, LANES), jnp.float32)
    for chunk, value in enumerate(values):
        sides = jnp.where(side_lanes(lane, chunk), turn(value, 2 * chunk), sides)
    return sides


def sides_kernel(winds_ref, _, sides_ref):
    sides_ref[...] = gather_sides(
        [tile_row(winds_ref, 1 - chunk % 2, chunk // 2) for chunk in range(CHUNKS)]
    )


def fold_parts(terms, count):
    folded = []
    for term in terms:
        for part in range(count):
            tile, group = divmod(part, 4)
            place = slice(tile * LANES, (tile + 1) * LANES)
            folded.append(tuple(None if x is None else turn(x[:, place], -32 * group) for x in term))
    return normalized(add_all(folded))


def turn(value, shift):
    return pltpu.roll(value, shift % LANES, 1) if shift % LANES else value


def row_bound(value):
    return jnp.broadcast_to(jnp.max(jnp.abs(value), axis=1, keepdims=True), value.shape)


def cut(value, bound, parts_ref, chunk):
    for part, piece in enumerate(split_parts(value, None, bound, X_PARTS)):
        parts_ref[part * SNAPS : (part + 1) * SNAPS, chunk * LANES : (chunk + 1) * LANES] = piece


def row_sum(blocks):
    groups = blocks[0][0].shape[0] // SNAPS
    return add_all(
        [
            tuple(None if x is None else x[part * SNAPS : (part + 1) * SNAPS] for x in block)
            for part in range(groups)
            for block in blocks
        ]
    )


def gram_of_parts(parts_ref):
    total = None
    for start in range(0, parts_ref.shape[1], 2 * LANES):
        piece = parts_ref[:, start : start + 2 * LANES]
        product = lax.dot_general(
            piece, piece, (((1,), (1,)), ((), ())), preferred_element_type=jnp.float32
        )
        total = (product, None) if total is None else add_terms(total, (product, None))
    return fold_parts([row_sum([total])], X_PARTS)


def tile_columns(winds_ref, low_lat_ref, high_lat_ref, table_ref, rows, sides):
    lane = lane_iota((SNAPS, LANES))
    inside = jnp.logical_and(lane > 0, lane < LANES - 1)

    def lon_diff(field, i):
        value = tile_row(winds_ref, field, i)
        after = jnp.where(lane == LANES - 1, 0.0, turn(value, -1))
        return after - jnp.where(lane == 0, 0.0, turn(value, 1))

    def weighted(field, i):
        if 0 <= i < ROWS:
            value = tile_row(winds_ref, field, i)
        else:
            value = (low_lat_ref if i < 0 else high_lat_ref)[field * SNAPS : (field + 1) * SNAPS, :]
        return table_ref[i + 1 : i + 2, :] * value

    def lat_diff(field, i):
        return weighted(field, i + 1) - weighted(field, i - 1)

    values = []
    for i in rows:
        scale = table_ref[16 + i : 17 + i, :]
        vorticity = (lon_diff(1, i) - lat_diff(0, i)) * scale
        divergence = (lon_diff(0, i) + lat_diff(1, i)) * scale
        for chunk, value in ((2 * i, vorticity), (2 * i + 1, divergence)):
            sides = jnp.where(side_lanes(lane, chunk), turn(value, 2 * chunk), sides)
            values.append(jnp.where(inside, value, 0.0))
    return values, sides


def largest_of(values):
    largest = jnp.abs(values[0])
    for value in values[1:]:
        largest = jnp.maximum(largest, jnp.abs(value))
    return row_bound(largest)


def inner_kernel(winds_ref, low_lat_ref, table_ref, parts_ref, pair_ref, sides_ref):
    none = jnp.zeros((SNAPS, LANES), jnp.float32)
    values, sides = tile_columns(winds_ref, low_lat_ref, None, table_ref, range(ROWS - 1), none)
    sides_ref[...] = sides
    bound = largest_of(values)
    for chunk, value in enumerate(values):
        cut(value, bound, parts_ref, chunk)
    pair_ref[0], pair_ref[1] = gram_of_parts(parts_ref)


def edge_kernel(
    winds_ref, low_lon_ref, high_lon_ref, table_ref, pair_ref, sides_ref, high_lat_ref, parts_ref, gram_ref
):
    lane = lane_iota((SNAPS, LANES))
    values, sides = tile_columns(winds_ref, None, high_lat_ref, table_ref, (ROWS - 1,), sides_ref[...])
    before, after = turn(low_lon_ref[...], 1), turn(high_lon_ref[...], -1)
    values.append(sides + jnp.where(lane % 2 == 0, -before, after) * table_ref[24:25, :])
    bound = largest_of(values)
    for chunk, value in enumerate(values):
        cut(value, bound, parts_ref, chunk)
    pair = normalized(add_terms(gram_of_parts(parts_ref), (pair_ref[0], pair_ref[1])))
    packed, last = pack_pair(pair)
    store_copies(gram_ref, [packed[r : r + 1, :] for r in range(8)] + [last])


def store_copies(ref, rows):
    copies = ref.shape[0] // PACKED
    for r, row in enumerate(rows):
        ref[pl.ds(r, copies, stride=PACKED), :] = jnp.broadcast_to(row[0:1, :], (copies, LANES))


def group_lane(shape):
    return lane_iota(shape) % 32


def pack_pair(pair):
    shape = (8, LANES)
    row, group = row_iota(shape), group_lane(shape)
    packed = None
    for b in range(4):
        merged = []
        for value, offset in zip(pair, (0, 16)):
            block = value[8 * b : 8 * b + 8]
            base = (8 * b - offset) % 32
            near = pltpu.roll(block, LANES - base, 1) if base else block
            block = jnp.where(row % 2 == 1, pltpu.roll(block, LANES - base - 1, 1), near)
            block = jnp.where(row % 4 >= 2, pltpu.roll(block, LANES - 2, 1), block)
            block = jnp.where(row >= 4, pltpu.roll(block, LANES - 4, 1), block)
            merged.append(block)
        block = jnp.where(group < 16, merged[0], merged[1])
        packed = block if packed is None else jnp.where(lane_iota(shape) < 32 * b, packed, block)
    half = (16, LANES)
    row, group = row_iota(half), group_lane(half)
    high = jnp.where(group == row, pltpu.roll(pair[0][:16], 16, 1), 0.0)
    low = jnp.where(group == row + 16, pair[1][:16], 0.0)
    return packed, jnp.sum(high + low, axis=0, keepdims=True)


def unpack_pair(rows):
    shape = (8, LANES)
    packed = rows[0]
    for r in range(1, 8):
        packed = jnp.where(row_iota(shape) == r, rows[r], packed)
    full = (SNAPS, LANES)
    row, lane = row_iota(full), lane_iota(full)
    distance = (lane - row) % 32
    last = jnp.concatenate([rows[8]] * 4, axis=0)
    result = []
    for offset in (0, 16):
        blocks = []
        for g in range(4):
            block = jnp.where(lane_iota(shape) < 16, pltpu.roll(packed, (-32 * g - offset) % LANES, 1), 0.0)
            blocks.append(pltpu.roll(block, 8 * g, 1, stride=1, stride_axis=0))
        right = jnp.concatenate(blocks, axis=0)
        right = jnp.where(lane < 32, right + pltpu.roll(right, LANES - 32, 1), 0.0)
        if offset:
            sides = jnp.where(row < 16, last, pltpu.roll(last, LANES - 16, 1))
        else:
            sides = jnp.where(row < 16, pltpu.roll(last, 16, 1), last)
        mirrored = jnp.concatenate([right, jnp.zeros((LANES - SNAPS, LANES), jnp.float32)], axis=0).T[:SNAPS]
        value = jnp.where(distance < 16, right, jnp.where(distance == 16, sides, mirrored))
        result.append(jnp.where(lane < 32, value, 0.0))
    return result


def add_pairs(ref):
    count = ref.shape[0] // PACKED
    group = group_lane((8, LANES))
    rows = []
    for r in range(PACKED):
        values = ref[pl.ds(r, count, stride=PACKED), :]
        if count % 8:
            values = jnp.concatenate([values, jnp.zeros((-count % 8, LANES), jnp.float32)], axis=0)
        terms = [(values[k : k + 8], None) for k in range(0, values.shape[0], 8)]
        total = add_all(terms)
        for shift in (4, 2, 1):
            other = tuple(None if x is None else pltpu.roll(x, shift, 0) for x in total)
            total = add_terms(total, other)
        low = pltpu.roll(total[0], LANES - 16, 1) + total[1]
        high = total[0] + low
        low = low - (high - total[0])
        rows.append(jnp.where(group < 16, high, pltpu.roll(low, 16, 1)))
    return rows


def merge_kernel(all_ref, out_ref):
    store_copies(out_ref, add_pairs(all_ref))


def factor_and_inverse(square):
    shape = (8, LANES)
    lane, row = lane_iota(shape), row_iota(shape)
    blocks = [
        jnp.where(lane == row + (32 + 8 * b), 1.0, square[8 * b : 8 * b + 8]) for b in range(4)
    ]
    upper, lower = [], []
    for b in range(4):
        columns = [
            [jnp.broadcast_to(block[:, 8 * b + w : 8 * b + w + 1], shape) for block in blocks[b:]]
            for w in range(8)
        ]
        rows = [jnp.broadcast_to(blocks[b][w : w + 1, :], shape) for w in range(8)]
        corner = [
            [jnp.broadcast_to(columns[t][0][w : w + 1, :], shape) if t >= w else None for t in range(8)]
            for w in range(8)
        ]
        pivots, done = corner[0][0], rows[0]
        for w in range(8):
            inverse = 1.0 / corner[w][w]
            for t in range(w + 1, 8):
                ratio = corner[w][t] * inverse
                rows[t] = rows[t] - ratio * rows[w]
                for s in range(t, 8):
                    corner[t][s] = corner[t][s] - ratio * corner[w][s]
            for i in range(1, 4 - b):
                left = columns[w][i] * inverse
                for t in range(w + 1, 8):
                    columns[t][i] = columns[t][i] - left * corner[w][t]
                blocks[b + i] = blocks[b + i] - left * rows[w]
            if w:
                pivots = jnp.where(row == w, corner[w][w], pivots)
                done = jnp.where(row == w, rows[w], done)
        scale = lax.rsqrt(pivots)
        scaled = done * (scale * (1.5 - 0.5 * pivots * scale * scale))
        upper.append(jnp.where(jnp.logical_and(lane >= row + 8 * b, lane < 32), scaled, 0.0))
        lower.append(jnp.where(lane < 32, pltpu.roll(scaled, LANES - 32, 1), 0.0))
    return jnp.concatenate(upper, axis=0), jnp.concatenate(lower, axis=0)


def product_of_parts(left, right):
    count = len(right)
    tiles = -(-count // 4)
    rows = jnp.concatenate(left, axis=0)
    columns = jnp.concatenate(list(right) + [jnp.zeros_like(right[0])] * (4 * tiles - count), axis=0)
    blocks = lax.dot_general(
        rows, columns, (((1,), (1,)), ((), ())), preferred_element_type=jnp.float32
    )
    lane = lane_iota((SNAPS, LANES))
    folded = fold_parts([row_sum([(blocks, None)])], count)
    return tuple(jnp.where(lane < 32, value, 0.0) for value in folded)


def exact_dot(left, right, contract):
    return lax.dot_general(
        left,
        right,
        (contract, ((), ())),
        precision=lax.Precision.HIGHEST,
        preferred_element_type=jnp.float32,
    )


def modes_kernel(root, all_ref, inner_ref, edge_ref, modes_ref, factor_ref):
    lane = lane_iota((SNAPS, LANES))
    high, low = unpack_pair(add_pairs(all_ref))
    first, first_inverse = factor_and_inverse(high)
    gram_parts = [p[:, :32] for p in split_parts(high, low, row_bound(high), G_PARTS)]
    inverse_parts = [p[:, :32] for p in split_parts(first_inverse, None, row_bound(first_inverse), X_PARTS)]
    half = product_of_parts(inverse_parts, gram_parts)
    half_parts = [p[:, :32] for p in split_parts(half[0], half[1], row_bound(half[0]), G_PARTS)]
    second_gram = product_of_parts(half_parts, inverse_parts)[0]
    second, second_inverse = factor_and_inverse(second_gram)
    factor_ref[...] = exact_dot(second[:, :32], first[:, :32], ((1,), (0,))) * (1.0 / root)
    weights = exact_dot(second_inverse[:, :32], first_inverse[:, :32], ((1,), (0,))) * root
    weights = jnp.concatenate([weights] * 4, axis=1)
    pieces = []
    for _ in range(3):
        piece = weights.astype(jnp.bfloat16)
        pieces.append(piece)
        weights = weights - piece.astype(jnp.float32)
    stacked = jnp.concatenate(pieces, axis=0)

    def times(parts):
        product = jnp.dot(stacked, parts, preferred_element_type=jnp.float32)
        return (product[64:96] + product[32:64]) + product[0:32]

    sides = times(edge_ref[:, 2 * LANES :])
    ends = jnp.logical_or(lane == 0, lane == LANES - 1)
    for i in range(ROWS):
        source, start = (inner_ref, i * 2 * LANES) if i < ROWS - 1 else (edge_ref, 0)
        value = times(source[:, start : start + 2 * LANES])
        for field in range(2):
            own = value[:, field * LANES : (field + 1) * LANES]
            place = pl.ds(field * ROWS + i, SNAPS, stride=CHUNKS)
            modes_ref[place, :] = jnp.where(ends, turn(sides, -2 * (2 * i + field)), own)


def call(kernel, shapes, operands, scratch=(), flops=10**8):
    return pl.pallas_call(
        kernel,
        out_shape=shapes,
        in_specs=[pl.BlockSpec(memory_space=pltpu.VMEM)] * len(operands),
        out_specs=[pl.BlockSpec(memory_space=pltpu.VMEM)] * len(shapes),
        scratch_shapes=list(scratch),
        compiler_params=pltpu.CompilerParams(vmem_limit_bytes=8 * 2**20),
        cost_estimate=pl.CostEstimate(flops=flops, bytes_accessed=2**19, transcendentals=0),
    )(*operands)


def shards(wind_u, wind_v):
    f32 = functools.partial(jax.ShapeDtypeStruct, dtype=jnp.float32)
    bf16 = functools.partial(jax.ShapeDtypeStruct, dtype=jnp.bfloat16)
    lat_axis, lon_axis = "lat", ("z", "core")
    lat_count, lon_count = lax.axis_size(lat_axis), lax.axis_size(lon_axis)
    near, far = lax.axis_size((lat_axis, "core")), lax.axis_size("z")
    winds = jnp.stack([wind_u, wind_v]).reshape(2 * SNAPS * ROWS, LANES)

    with jax.named_scope("halo"):
        up = [(i, i + 1) for i in range(lat_count - 1)]
        around = [(i, (i + 1) % lon_count) for i in range(lon_count)]
        back = lambda pairs: [(target, source) for source, target in pairs]
        north, south = call(rows_kernel, [f32((2 * SNAPS, LANES))] * 2, (winds,))
        low_lat = lax.ppermute(south, lat_axis, up)
        high_lat = lax.ppermute(north, lat_axis, back(up))
        (sides,) = call(sides_kernel, [f32((SNAPS, LANES))], (winds, low_lat))
        low_lon = lax.ppermute(sides, lon_axis, around)
        high_lon = lax.ppermute(sides, lon_axis, back(around))

    with jax.named_scope("table"):
        step = 2.0 * math.pi / (lon_count * LANES)
        line, lane = row_iota((32, LANES)), lane_iota((32, LANES))
        first_row = lax.axis_index(lat_axis) * ROWS
        offset = jnp.where(line < 16, line - 1, jnp.where(line < 24, line - 16, (lane + 1) % LANES // 4))
        index = (first_row + offset).astype(jnp.float32)
        cosine = jnp.cos((index + 0.5 - lat_count * ROWS / 2) * step)
        table = jnp.where(line < 16, cosine, 0.5 / jnp.sqrt(cosine))

    with jax.named_scope("gram"):
        height = X_PARTS * SNAPS
        inner_parts, pair, sides = call(
            inner_kernel,
            [bf16((height, 2 * (ROWS - 1) * LANES)), f32((2, SNAPS, LANES)), f32((SNAPS, LANES))],
            (winds, low_lat, table),
            flops=2 * 10**9,
        )
        edge_parts, gram = call(
            edge_kernel,
            [bf16((height, 3 * LANES)), f32((near * PACKED, LANES))],
            (winds, low_lon, high_lon, table, pair, sides, high_lat),
        )

    def exchange(copies, axis):
        flat = copies.reshape(-1, 1, PACKED * LANES)
        return lax.all_to_all(flat, axis, 0, 0, tiled=True).reshape(copies.shape)

    with jax.named_scope("sum_near"):
        gathered = exchange(gram, (lat_axis, "core"))
        (gram,) = call(merge_kernel, [f32((far * PACKED, LANES))], (gathered,))
    with jax.named_scope("sum_far"):
        gathered = exchange(gram, "z")

    with jax.named_scope("modes"):
        root = math.sqrt(lat_count * lon_count * CHUNKS * LANES)
        modes, factor = call(
            functools.partial(modes_kernel, root),
            [f32((SNAPS * CHUNKS, LANES)), f32((SNAPS, SNAPS))],
            (gathered, inner_parts, edge_parts),
        )
    return modes.reshape(SNAPS, 2, ROWS, LANES), factor


def solution(mesh):
    lat_count, lon_count = mesh.devices.shape
    inner = Mesh(mesh.devices.reshape(lat_count, lon_count // 2, 2), ("lat", "z", "core"))
    spec = P(None, "lat", ("z", "core"))
    return jax.shard_map(
        shards,
        mesh=inner,
        in_specs=(spec, spec),
        out_specs=(P(None, None, "lat", ("z", "core")), P()),
        check_vma=False,
    )
```

```python
import functools
import math

import jax
import jax.numpy as jnp
from jax import lax
from jax.experimental import pallas as pl
from jax.experimental.pallas import tpu as pltpu
from jax.sharding import Mesh, PartitionSpec as P

SNAPS = 32
ROWS = 8
LANES = 128
CHUNKS = 2 * ROWS
X_PARTS = 4
G_PARTS = 5
EDGES = (0, ROWS - 1)
INNER = tuple(range(1, ROWS - 1))
PACKED = 9


def two_sum(a, b):
    total = a + b
    part = total - a
    return total, (a - (total - part)) + (b - part)


def add_terms(a, b):
    total, error = two_sum(a[0], b[0])
    for known in (a[1], b[1]):
        if known is not None:
            error = error + known
    return total, error


def add_all(terms):
    while len(terms) > 1:
        merged = [add_terms(a, b) for a, b in zip(terms[::2], terms[1::2])]
        terms = merged + terms[2 * len(merged) :]
    return terms[0]


def normalized(term):
    high = term[0] + term[1]
    return high, term[1] - (high - term[0])


def split_parts(value, low, bound, count):
    parts = []
    grid = bound * 2.0**17
    for index in range(count):
        part = (value + grid) - grid
        parts.append(part.astype(jnp.bfloat16))
        value = value - part
        if low is not None and index == 2:
            value = value + low
        grid = grid * 2.0**-8
    return parts


def lane_iota(shape):
    return lax.broadcasted_iota(jnp.int32, shape, 1)


def row_iota(shape):
    return lax.broadcasted_iota(jnp.int32, shape, 0)


def tile_row(ref, field, index):
    return ref[pl.ds(field * SNAPS * ROWS + index, SNAPS, stride=ROWS), :]


def rows_kernel(winds_ref, odd_ref, wide_ref, close_ref):
    odd = odd_ref[0:1, :] > 0.5
    for field in range(2):
        place = slice(field * SNAPS, (field + 1) * SNAPS)
        north, south = tile_row(winds_ref, field, 0), tile_row(winds_ref, field, ROWS - 1)
        wide_ref[place, :] = jnp.where(odd, south, north)
        close_ref[place, :] = jnp.where(odd, north, south)


def side_lanes(lane, chunk):
    return jnp.logical_or(lane == 2 * chunk, lane == (2 * chunk - 1) % LANES)


def gather_sides(values):
    lane = lane_iota((SNAPS, LANES))
    sides = jnp.zeros((SNAPS, LANES), jnp.float32)
    for chunk, value in enumerate(values):
        sides = jnp.where(side_lanes(lane, chunk), turn(value, 2 * chunk), sides)
    return sides


def sides_kernel(winds_ref, _, sides_ref):
    sides_ref[...] = gather_sides(
        [tile_row(winds_ref, 1 - chunk % 2, chunk // 2) for chunk in range(CHUNKS)]
    )


def fold_parts(terms, count):
    folded = []
    for term in terms:
        for part in range(count):
            tile, group = divmod(part, 4)
            place = slice(tile * LANES, (tile + 1) * LANES)
            folded.append(tuple(None if x is None else turn(x[:, place], -32 * group) for x in term))
    return normalized(add_all(folded))


def turn(value, shift):
    return pltpu.roll(value, shift % LANES, 1) if shift % LANES else value


def row_bound(value):
    return jnp.broadcast_to(jnp.max(jnp.abs(value), axis=1, keepdims=True), value.shape)


def cut(value, bound, parts_ref, chunk):
    for part, piece in enumerate(split_parts(value, None, bound, X_PARTS)):
        parts_ref[part * SNAPS : (part + 1) * SNAPS, chunk * LANES : (chunk + 1) * LANES] = piece


def row_sum(blocks):
    groups = blocks[0][0].shape[0] // SNAPS
    return add_all(
        [
            tuple(None if x is None else x[part * SNAPS : (part + 1) * SNAPS] for x in block)
            for part in range(groups)
            for block in blocks
        ]
    )


def gram_of_parts(parts_ref):
    total = None
    for start in range(0, parts_ref.shape[1], 2 * LANES):
        piece = parts_ref[:, start : start + 2 * LANES]
        product = lax.dot_general(
            piece, piece, (((1,), (1,)), ((), ())), preferred_element_type=jnp.float32
        )
        total = (product, None) if total is None else add_terms(total, (product, None))
    return fold_parts([row_sum([total])], X_PARTS)


def tile_columns(winds_ref, lat_halos, table_ref, rows, sides):
    lane = lane_iota((SNAPS, LANES))
    inside = jnp.logical_and(lane > 0, lane < LANES - 1)

    def lon_diff(field, i):
        value = tile_row(winds_ref, field, i)
        after = jnp.where(lane == LANES - 1, 0.0, turn(value, -1))
        return after - jnp.where(lane == 0, 0.0, turn(value, 1))

    def weighted(field, i):
        if 0 <= i < ROWS:
            value = tile_row(winds_ref, field, i)
        else:
            value = lat_halos[i >= ROWS][field * SNAPS : (field + 1) * SNAPS, :]
        return table_ref[i + 1 : i + 2, :] * value

    def lat_diff(field, i):
        return weighted(field, i + 1) - weighted(field, i - 1)

    values = []
    for i in rows:
        scale = table_ref[16 + i : 17 + i, :]
        vorticity = (lon_diff(1, i) - lat_diff(0, i)) * scale
        divergence = (lon_diff(0, i) + lat_diff(1, i)) * scale
        for chunk, value in ((2 * i, vorticity), (2 * i + 1, divergence)):
            sides = jnp.where(side_lanes(lane, chunk), turn(value, 2 * chunk), sides)
            values.append(jnp.where(inside, value, 0.0))
    return values, sides


def largest_of(values):
    largest = jnp.abs(values[0])
    for value in values[1:]:
        largest = jnp.maximum(largest, jnp.abs(value))
    return row_bound(largest)


def inner_kernel(winds_ref, table_ref, parts_ref, pair_ref, sides_ref):
    none = jnp.zeros((SNAPS, LANES), jnp.float32)
    values, sides = tile_columns(winds_ref, None, table_ref, INNER, none)
    sides_ref[...] = sides
    bound = largest_of(values)
    for chunk, value in enumerate(values):
        cut(value, bound, parts_ref, chunk)
    pair_ref[0], pair_ref[1] = gram_of_parts(parts_ref)


def edge_kernel(
    winds_ref, low_lon_ref, high_lon_ref, table_ref, pair_ref, sides_ref, odd_ref, wide_ref, close_ref, parts_ref, gram_ref
):
    lane = lane_iota((SNAPS, LANES))
    odd = odd_ref[0:1, :] > 0.5
    wide, close = wide_ref[...], close_ref[...]
    lat_halos = jnp.where(odd, close, wide), jnp.where(odd, wide, close)
    values, sides = tile_columns(winds_ref, lat_halos, table_ref, EDGES, sides_ref[...])
    before, after = turn(low_lon_ref[...], 1), turn(high_lon_ref[...], -1)
    values.append(sides + jnp.where(lane % 2 == 0, -before, after) * table_ref[24:25, :])
    bound = largest_of(values)
    for chunk, value in enumerate(values):
        cut(value, bound, parts_ref, chunk)
    pair = normalized(add_terms(gram_of_parts(parts_ref), (pair_ref[0], pair_ref[1])))
    packed, last = pack_pair(pair)
    store_copies(gram_ref, [packed[r : r + 1, :] for r in range(8)] + [last])


def store_copies(ref, rows):
    copies = ref.shape[0] // PACKED
    for r, row in enumerate(rows):
        ref[pl.ds(r, copies, stride=PACKED), :] = jnp.broadcast_to(row[0:1, :], (copies, LANES))


def group_lane(shape):
    return lane_iota(shape) % 32


def pack_pair(pair):
    shape = (8, LANES)
    row, group = row_iota(shape), group_lane(shape)
    packed = None
    for b in range(4):
        merged = []
        for value, offset in zip(pair, (0, 16)):
            block = value[8 * b : 8 * b + 8]
            base = (8 * b - offset) % 32
            near = pltpu.roll(block, LANES - base, 1) if base else block
            block = jnp.where(row % 2 == 1, pltpu.roll(block, LANES - base - 1, 1), near)
            block = jnp.where(row % 4 >= 2, pltpu.roll(block, LANES - 2, 1), block)
            block = jnp.where(row >= 4, pltpu.roll(block, LANES - 4, 1), block)
            merged.append(block)
        block = jnp.where(group < 16, merged[0], merged[1])
        packed = block if packed is None else jnp.where(lane_iota(shape) < 32 * b, packed, block)
    half = (16, LANES)
    row, group = row_iota(half), group_lane(half)
    high = jnp.where(group == row, pltpu.roll(pair[0][:16], 16, 1), 0.0)
    low = jnp.where(group == row + 16, pair[1][:16], 0.0)
    return packed, jnp.sum(high + low, axis=0, keepdims=True)


def unpack_pair(rows):
    shape = (8, LANES)
    packed = rows[0]
    for r in range(1, 8):
        packed = jnp.where(row_iota(shape) == r, rows[r], packed)
    full = (SNAPS, LANES)
    row, lane = row_iota(full), lane_iota(full)
    distance = (lane - row) % 32
    last = jnp.concatenate([rows[8]] * 4, axis=0)
    result = []
    for offset in (0, 16):
        blocks = []
        for g in range(4):
            block = jnp.where(lane_iota(shape) < 16, pltpu.roll(packed, (-32 * g - offset) % LANES, 1), 0.0)
            blocks.append(pltpu.roll(block, 8 * g, 1, stride=1, stride_axis=0))
        right = jnp.concatenate(blocks, axis=0)
        right = jnp.where(lane < 32, right + pltpu.roll(right, LANES - 32, 1), 0.0)
        if offset:
            sides = jnp.where(row < 16, last, pltpu.roll(last, LANES - 16, 1))
        else:
            sides = jnp.where(row < 16, pltpu.roll(last, 16, 1), last)
        mirrored = jnp.concatenate([right, jnp.zeros((LANES - SNAPS, LANES), jnp.float32)], axis=0).T[:SNAPS]
        value = jnp.where(distance < 16, right, jnp.where(distance == 16, sides, mirrored))
        result.append(jnp.where(lane < 32, value, 0.0))
    return result


def add_pairs(ref):
    count = ref.shape[0] // PACKED
    group = group_lane((8, LANES))
    rows = []
    for r in range(PACKED):
        values = ref[pl.ds(r, count, stride=PACKED), :]
        if count % 8:
            values = jnp.concatenate([values, jnp.zeros((-count % 8, LANES), jnp.float32)], axis=0)
        terms = [(values[k : k + 8], None) for k in range(0, values.shape[0], 8)]
        total = add_all(terms)
        for shift in (4, 2, 1):
            other = tuple(None if x is None else pltpu.roll(x, shift, 0) for x in total)
            total = add_terms(total, other)
        low = pltpu.roll(total[0], LANES - 16, 1) + total[1]
        high = total[0] + low
        low = low - (high - total[0])
        rows.append(jnp.where(group < 16, high, pltpu.roll(low, 16, 1)))
    return rows


def merge_kernel(all_ref, out_ref):
    store_copies(out_ref, add_pairs(all_ref))


def factor_and_inverse(square):
    shape = (8, LANES)
    lane, row = lane_iota(shape), row_iota(shape)
    blocks = [
        jnp.where(lane == row + (32 + 8 * b), 1.0, square[8 * b : 8 * b + 8]) for b in range(4)
    ]
    upper, lower = [], []
    for b in range(4):
        columns = [
            [jnp.broadcast_to(block[:, 8 * b + w : 8 * b + w + 1], shape) for block in blocks[b:]]
            for w in range(8)
        ]
        rows = [jnp.broadcast_to(blocks[b][w : w + 1, :], shape) for w in range(8)]
        corner = [
            [jnp.broadcast_to(columns[t][0][w : w + 1, :], shape) if t >= w else None for t in range(8)]
            for w in range(8)
        ]
        pivots, done = corner[0][0], rows[0]
        for w in range(8):
            inverse = 1.0 / corner[w][w]
            for t in range(w + 1, 8):
                ratio = corner[w][t] * inverse
                rows[t] = rows[t] - ratio * rows[w]
                for s in range(t, 8):
                    corner[t][s] = corner[t][s] - ratio * corner[w][s]
            for i in range(1, 4 - b):
                left = columns[w][i] * inverse
                for t in range(w + 1, 8):
                    columns[t][i] = columns[t][i] - left * corner[w][t]
                blocks[b + i] = blocks[b + i] - left * rows[w]
            if w:
                pivots = jnp.where(row == w, corner[w][w], pivots)
                done = jnp.where(row == w, rows[w], done)
        scale = lax.rsqrt(pivots)
        scaled = done * (scale * (1.5 - 0.5 * pivots * scale * scale))
        upper.append(jnp.where(jnp.logical_and(lane >= row + 8 * b, lane < 32), scaled, 0.0))
        lower.append(jnp.where(lane < 32, pltpu.roll(scaled, LANES - 32, 1), 0.0))
    return jnp.concatenate(upper, axis=0), jnp.concatenate(lower, axis=0)


def product_of_parts(left, right):
    count = len(right)
    tiles = -(-count // 4)
    rows = jnp.concatenate(left, axis=0)
    columns = jnp.concatenate(list(right) + [jnp.zeros_like(right[0])] * (4 * tiles - count), axis=0)
    blocks = lax.dot_general(
        rows, columns, (((1,), (1,)), ((), ())), preferred_element_type=jnp.float32
    )
    lane = lane_iota((SNAPS, LANES))
    folded = fold_parts([row_sum([(blocks, None)])], count)
    return tuple(jnp.where(lane < 32, value, 0.0) for value in folded)


def exact_dot(left, right, contract):
    return lax.dot_general(
        left,
        right,
        (contract, ((), ())),
        precision=lax.Precision.HIGHEST,
        preferred_element_type=jnp.float32,
    )


def modes_kernel(root, all_ref, inner_ref, edge_ref, modes_ref, factor_ref):
    lane = lane_iota((SNAPS, LANES))
    high, low = unpack_pair(add_pairs(all_ref))
    first, first_inverse = factor_and_inverse(high)
    gram_parts = [p[:, :32] for p in split_parts(high, low, row_bound(high), G_PARTS)]
    inverse_parts = [p[:, :32] for p in split_parts(first_inverse, None, row_bound(first_inverse), X_PARTS)]
    half = product_of_parts(inverse_parts, gram_parts)
    half_parts = [p[:, :32] for p in split_parts(half[0], half[1], row_bound(half[0]), G_PARTS)]
    second_gram = product_of_parts(half_parts, inverse_parts)[0]
    second, second_inverse = factor_and_inverse(second_gram)
    factor_ref[...] = exact_dot(second[:, :32], first[:, :32], ((1,), (0,))) * (1.0 / root)
    weights = exact_dot(second_inverse[:, :32], first_inverse[:, :32], ((1,), (0,))) * root
    weights = jnp.concatenate([weights] * 4, axis=1)
    pieces = []
    for _ in range(3):
        piece = weights.astype(jnp.bfloat16)
        pieces.append(piece)
        weights = weights - piece.astype(jnp.float32)
    stacked = jnp.concatenate(pieces, axis=0)

    def times(parts):
        product = jnp.dot(stacked, parts, preferred_element_type=jnp.float32)
        return (product[64:96] + product[32:64]) + product[0:32]

    sides = times(edge_ref[:, 2 * len(EDGES) * LANES :])
    ends = jnp.logical_or(lane == 0, lane == LANES - 1)
    for parts_ref, rows in ((edge_ref, EDGES), (inner_ref, INNER)):
        for index, i in enumerate(rows):
            value = times(parts_ref[:, index * 2 * LANES : (index + 1) * 2 * LANES])
            for field in range(2):
                own = value[:, field * LANES : (field + 1) * LANES]
                place = pl.ds(field * ROWS + i, SNAPS, stride=CHUNKS)
                modes_ref[place, :] = jnp.where(ends, turn(sides, -2 * (2 * i + field)), own)


def call(kernel, shapes, operands, scratch=(), flops=10**8):
    return pl.pallas_call(
        kernel,
        out_shape=shapes,
        in_specs=[pl.BlockSpec(memory_space=pltpu.VMEM)] * len(operands),
        out_specs=[pl.BlockSpec(memory_space=pltpu.VMEM)] * len(shapes),
        scratch_shapes=list(scratch),
        compiler_params=pltpu.CompilerParams(vmem_limit_bytes=8 * 2**20),
        cost_estimate=pl.CostEstimate(flops=flops, bytes_accessed=2**19, transcendentals=0),
    )(*operands)


def shards(wind_u, wind_v):
    f32 = functools.partial(jax.ShapeDtypeStruct, dtype=jnp.float32)
    bf16 = functools.partial(jax.ShapeDtypeStruct, dtype=jnp.bfloat16)
    lat_axis, lon_axis = "lat", ("z", "core")
    lat_count, lon_count = lax.axis_size(lat_axis), lax.axis_size(lon_axis)
    near, far = lax.axis_size((lat_axis, "core")), lax.axis_size("z")
    winds = jnp.stack([wind_u, wind_v]).reshape(2 * SNAPS * ROWS, LANES)

    with jax.named_scope("halo"):
        around = [(i, (i + 1) % lon_count) for i in range(lon_count)]
        back = lambda pairs: [(target, source) for source, target in pairs]
        pairing = lambda first: [(i, i + 1) for i in range(first, lat_count - 1, 2)]
        odd = jnp.full((8, LANES), lax.axis_index(lat_axis) % 2, jnp.float32)
        facing = call(rows_kernel, [f32((2 * SNAPS, LANES))] * 2, (winds, odd))
        wide, close = (
            lax.ppermute(row, lat_axis, pairing(first) + back(pairing(first)))
            for row, first in zip(facing, (1, 0))
        )
        (sides,) = call(sides_kernel, [f32((SNAPS, LANES))], (winds, wide))
        low_lon = lax.ppermute(sides, lon_axis, around)
        high_lon = lax.ppermute(sides, lon_axis, back(around))

    with jax.named_scope("table"):
        step = 2.0 * math.pi / (lon_count * LANES)
        line, lane = row_iota((32, LANES)), lane_iota((32, LANES))
        first_row = lax.axis_index(lat_axis) * ROWS
        offset = jnp.where(line < 16, line - 1, jnp.where(line < 24, line - 16, (lane + 1) % LANES // 4))
        index = (first_row + offset).astype(jnp.float32)
        cosine = jnp.cos((index + 0.5 - lat_count * ROWS / 2) * step)
        table = jnp.where(line < 16, cosine, 0.5 / jnp.sqrt(cosine))

    with jax.named_scope("gram"):
        height = X_PARTS * SNAPS
        inner_parts, pair, sides = call(
            inner_kernel,
            [bf16((height, 2 * len(INNER) * LANES)), f32((2, SNAPS, LANES)), f32((SNAPS, LANES))],
            (winds, table),
            flops=2 * 10**9,
        )
        edge_parts, gram = call(
            edge_kernel,
            [bf16((height, (2 * len(EDGES) + 1) * LANES)), f32((near * PACKED, LANES))],
            (winds, low_lon, high_lon, table, pair, sides, odd, wide, close),
        )

    def exchange(copies, axis):
        flat = copies.reshape(-1, 1, PACKED * LANES)
        return lax.all_to_all(flat, axis, 0, 0, tiled=True).reshape(copies.shape)

    with jax.named_scope("sum_near"):
        gathered = exchange(gram, (lat_axis, "core"))
        (gram,) = call(merge_kernel, [f32((far * PACKED, LANES))], (gathered,))
    with jax.named_scope("sum_far"):
        gathered = exchange(gram, "z")

    with jax.named_scope("modes"):
        root = math.sqrt(lat_count * lon_count * CHUNKS * LANES)
        modes, factor = call(
            functools.partial(modes_kernel, root),
            [f32((SNAPS * CHUNKS, LANES)), f32((SNAPS, SNAPS))],
            (gathered, inner_parts, edge_parts),
        )
    return modes.reshape(SNAPS, 2, ROWS, LANES), factor


def solution(mesh):
    lat_count, lon_count = mesh.devices.shape
    inner = Mesh(mesh.devices.reshape(lat_count, lon_count // 2, 2), ("lat", "z", "core"))
    spec = P(None, "lat", ("z", "core"))
    return jax.shard_map(
        shards,
        mesh=inner,
        in_specs=(spec, spec),
        out_specs=(P(None, None, "lat", ("z", "core")), P()),
        check_vma=False,
    )
```

```python
import functools
import math

import jax
import jax.numpy as jnp
from jax import lax
from jax.experimental import pallas as pl
from jax.experimental.pallas import tpu as pltpu
from jax.sharding import Mesh, PartitionSpec as P

SNAPS = 32
ROWS = 8
LANES = 128
CHUNKS = 2 * ROWS
X_PARTS = 4
G_PARTS = 5
EDGES = (0, ROWS - 1)
INNER = tuple(range(1, ROWS - 1))
PACKED = 9


def two_sum(a, b):
    total = a + b
    part = total - a
    return total, (a - (total - part)) + (b - part)


def add_terms(a, b):
    total, error = two_sum(a[0], b[0])
    for known in (a[1], b[1]):
        if known is not None:
            error = error + known
    return total, error


def add_all(terms):
    while len(terms) > 1:
        merged = [add_terms(a, b) for a, b in zip(terms[::2], terms[1::2])]
        terms = merged + terms[2 * len(merged) :]
    return terms[0]


def normalized(term):
    high = term[0] + term[1]
    return high, term[1] - (high - term[0])


def split_parts(value, low, bound, count):
    parts = []
    grid = bound * 2.0**17
    for index in range(count):
        part = (value + grid) - grid
        parts.append(part.astype(jnp.bfloat16))
        value = value - part
        if low is not None and index == 2:
            value = value + low
        grid = grid * 2.0**-8
    return parts


def lane_iota(shape):
    return lax.broadcasted_iota(jnp.int32, shape, 1)


def row_iota(shape):
    return lax.broadcasted_iota(jnp.int32, shape, 0)


def tile_row(ref, field, index):
    return ref[pl.ds(field * SNAPS * ROWS + index, SNAPS, stride=ROWS), :]


def rows_kernel(winds_ref, odd_ref, wide_ref, close_ref):
    odd = odd_ref[0:1, :] > 0.5
    for field in range(2):
        place = slice(field * SNAPS, (field + 1) * SNAPS)
        north, south = tile_row(winds_ref, field, 0), tile_row(winds_ref, field, ROWS - 1)
        wide_ref[place, :] = jnp.where(odd, south, north)
        close_ref[place, :] = jnp.where(odd, north, south)


def side_lanes(lane, chunk):
    return jnp.logical_or(lane == 2 * chunk, lane == (2 * chunk - 1) % LANES)


def gather_sides(values):
    lane = lane_iota((SNAPS, LANES))
    sides = jnp.zeros((SNAPS, LANES), jnp.float32)
    for chunk, value in enumerate(values):
        sides = jnp.where(side_lanes(lane, chunk), turn(value, 2 * chunk), sides)
    return sides


def sides_kernel(winds_ref, _, sides_ref):
    sides_ref[...] = gather_sides(
        [tile_row(winds_ref, 1 - chunk % 2, chunk // 2) for chunk in range(CHUNKS)]
    )


def fold_parts(terms, count):
    folded = []
    for term in terms:
        for part in range(count):
            tile, group = divmod(part, 4)
            place = slice(tile * LANES, (tile + 1) * LANES)
            folded.append(tuple(None if x is None else turn(x[:, place], -32 * group) for x in term))
    return normalized(add_all(folded))


def turn(value, shift):
    return pltpu.roll(value, shift % LANES, 1) if shift % LANES else value


def row_bound(value):
    return jnp.broadcast_to(jnp.max(jnp.abs(value), axis=1, keepdims=True), value.shape)


def cut(value, bound, parts_ref, chunk):
    for part, piece in enumerate(split_parts(value, None, bound, X_PARTS)):
        parts_ref[part * SNAPS : (part + 1) * SNAPS, chunk * LANES : (chunk + 1) * LANES] = piece


def row_sum(blocks):
    groups = blocks[0][0].shape[0] // SNAPS
    return add_all(
        [
            tuple(None if x is None else x[part * SNAPS : (part + 1) * SNAPS] for x in block)
            for part in range(groups)
            for block in blocks
        ]
    )


def gram_of_parts(parts_ref):
    total = None
    for start in range(0, parts_ref.shape[1], 2 * LANES):
        piece = parts_ref[:, start : start + 2 * LANES]
        product = lax.dot_general(
            piece, piece, (((1,), (1,)), ((), ())), preferred_element_type=jnp.float32
        )
        total = (product, None) if total is None else add_terms(total, (product, None))
    return fold_parts([row_sum([total])], X_PARTS)


def tile_columns(winds_ref, lat_halos, table_ref, rows, sides):
    lane = lane_iota((SNAPS, LANES))
    inside = jnp.logical_and(lane > 0, lane < LANES - 1)

    def lon_diff(field, i):
        value = tile_row(winds_ref, field, i)
        after = jnp.where(lane == LANES - 1, 0.0, turn(value, -1))
        return after - jnp.where(lane == 0, 0.0, turn(value, 1))

    def weighted(field, i):
        if 0 <= i < ROWS:
            value = tile_row(winds_ref, field, i)
        else:
            value = lat_halos[i >= ROWS][field * SNAPS : (field + 1) * SNAPS, :]
        return table_ref[i + 1 : i + 2, :] * value

    def lat_diff(field, i):
        return weighted(field, i + 1) - weighted(field, i - 1)

    values = []
    for i in rows:
        scale = table_ref[16 + i : 17 + i, :]
        vorticity = (lon_diff(1, i) - lat_diff(0, i)) * scale
        divergence = (lon_diff(0, i) + lat_diff(1, i)) * scale
        for chunk, value in ((2 * i, vorticity), (2 * i + 1, divergence)):
            sides = jnp.where(side_lanes(lane, chunk), turn(value, 2 * chunk), sides)
            values.append(jnp.where(inside, value, 0.0))
    return values, sides


def largest_of(values):
    largest = jnp.abs(values[0])
    for value in values[1:]:
        largest = jnp.maximum(largest, jnp.abs(value))
    return row_bound(largest)


def inner_kernel(winds_ref, table_ref, parts_ref, pair_ref, sides_ref):
    none = jnp.zeros((SNAPS, LANES), jnp.float32)
    values, sides = tile_columns(winds_ref, None, table_ref, INNER, none)
    sides_ref[...] = sides
    bound = largest_of(values)
    for chunk, value in enumerate(values):
        cut(value, bound, parts_ref, chunk)
    pair_ref[0], pair_ref[1] = gram_of_parts(parts_ref)


def edge_kernel(
    winds_ref, low_lon_ref, high_lon_ref, table_ref, pair_ref, sides_ref, odd_ref, wide_ref, close_ref, parts_ref, gram_ref
):
    lane = lane_iota((SNAPS, LANES))
    odd = odd_ref[0:1, :] > 0.5
    wide, close = wide_ref[...], close_ref[...]
    lat_halos = jnp.where(odd, close, wide), jnp.where(odd, wide, close)
    values, sides = tile_columns(winds_ref, lat_halos, table_ref, EDGES, sides_ref[...])
    before, after = turn(low_lon_ref[...], 1), turn(high_lon_ref[...], -1)
    values.append(sides + jnp.where(lane % 2 == 0, -before, after) * table_ref[24:25, :])
    bound = largest_of(values)
    for chunk, value in enumerate(values):
        cut(value, bound, parts_ref, chunk)
    pair = normalized(add_terms(gram_of_parts(parts_ref), (pair_ref[0], pair_ref[1])))
    packed, last = pack_pair(pair)
    store_copies(gram_ref, [packed[r : r + 1, :] for r in range(8)] + [last])


def store_copies(ref, rows):
    copies = ref.shape[0] // PACKED
    for r, row in enumerate(rows):
        ref[pl.ds(r, copies, stride=PACKED), :] = jnp.broadcast_to(row[0:1, :], (copies, LANES))


def group_lane(shape):
    return lane_iota(shape) % 32


def pack_pair(pair):
    shape = (8, LANES)
    row, group = row_iota(shape), group_lane(shape)
    packed = None
    for b in range(4):
        merged = []
        for value, offset in zip(pair, (0, 16)):
            block = value[8 * b : 8 * b + 8]
            base = (8 * b - offset) % 32
            near = pltpu.roll(block, LANES - base, 1) if base else block
            block = jnp.where(row % 2 == 1, pltpu.roll(block, LANES - base - 1, 1), near)
            block = jnp.where(row % 4 >= 2, pltpu.roll(block, LANES - 2, 1), block)
            block = jnp.where(row >= 4, pltpu.roll(block, LANES - 4, 1), block)
            merged.append(block)
        block = jnp.where(group < 16, merged[0], merged[1])
        packed = block if packed is None else jnp.where(lane_iota(shape) < 32 * b, packed, block)
    half = (16, LANES)
    row, group = row_iota(half), group_lane(half)
    high = jnp.where(group == row, pltpu.roll(pair[0][:16], 16, 1), 0.0)
    low = jnp.where(group == row + 16, pair[1][:16], 0.0)
    return packed, jnp.sum(high + low, axis=0, keepdims=True)


def unpack_pair(rows):
    shape = (8, LANES)
    packed = rows[0]
    for r in range(1, 8):
        packed = jnp.where(row_iota(shape) == r, rows[r], packed)
    full = (SNAPS, LANES)
    row, lane = row_iota(full), lane_iota(full)
    distance = (lane - row) % 32
    last = jnp.concatenate([rows[8]] * 4, axis=0)
    result = []
    for offset in (0, 16):
        blocks = []
        for g in range(4):
            block = jnp.where(lane_iota(shape) < 16, pltpu.roll(packed, (-32 * g - offset) % LANES, 1), 0.0)
            blocks.append(pltpu.roll(block, 8 * g, 1, stride=1, stride_axis=0))
        right = jnp.concatenate(blocks, axis=0)
        right = jnp.where(lane < 32, right + pltpu.roll(right, LANES - 32, 1), 0.0)
        if offset:
            sides = jnp.where(row < 16, last, pltpu.roll(last, LANES - 16, 1))
        else:
            sides = jnp.where(row < 16, pltpu.roll(last, 16, 1), last)
        mirrored = jnp.concatenate([right, jnp.zeros((LANES - SNAPS, LANES), jnp.float32)], axis=0).T[:SNAPS]
        value = jnp.where(distance < 16, right, jnp.where(distance == 16, sides, mirrored))
        result.append(jnp.where(lane < 32, value, 0.0))
    return result


def add_pairs(ref):
    count = ref.shape[0] // PACKED
    group = group_lane((8, LANES))
    rows = []
    for r in range(PACKED):
        values = ref[pl.ds(r, count, stride=PACKED), :]
        if count % 8:
            values = jnp.concatenate([values, jnp.zeros((-count % 8, LANES), jnp.float32)], axis=0)
        terms = [(values[k : k + 8], None) for k in range(0, values.shape[0], 8)]
        total = add_all(terms)
        for shift in (4, 2, 1):
            other = tuple(None if x is None else pltpu.roll(x, shift, 0) for x in total)
            total = add_terms(total, other)
        low = pltpu.roll(total[0], LANES - 16, 1) + total[1]
        high = total[0] + low
        low = low - (high - total[0])
        rows.append(jnp.where(group < 16, high, pltpu.roll(low, 16, 1)))
    return rows


def merge_kernel(all_ref, out_ref):
    store_copies(out_ref, add_pairs(all_ref))


def factor_and_inverse(square):
    shape = (8, LANES)
    lane, row = lane_iota(shape), row_iota(shape)
    blocks = [
        jnp.where(lane == row + (32 + 8 * b), 1.0, square[8 * b : 8 * b + 8]) for b in range(4)
    ]
    upper, lower = [], []
    for b in range(4):
        columns = [
            [jnp.broadcast_to(block[:, 8 * b + w : 8 * b + w + 1], shape) for block in blocks[b:]]
            for w in range(8)
        ]
        rows = [jnp.broadcast_to(blocks[b][w : w + 1, :], shape) for w in range(8)]
        corner = [
            [jnp.broadcast_to(columns[t][0][w : w + 1, :], shape) if t >= w else None for t in range(8)]
            for w in range(8)
        ]
        pivots, done = corner[0][0], rows[0]
        for w in range(8):
            inverse = 1.0 / corner[w][w]
            for t in range(w + 1, 8):
                ratio = corner[w][t] * inverse
                rows[t] = rows[t] - ratio * rows[w]
                for s in range(t, 8):
                    corner[t][s] = corner[t][s] - ratio * corner[w][s]
            for i in range(1, 4 - b):
                left = columns[w][i] * inverse
                for t in range(w + 1, 8):
                    columns[t][i] = columns[t][i] - left * corner[w][t]
                blocks[b + i] = blocks[b + i] - left * rows[w]
            if w:
                pivots = jnp.where(row == w, corner[w][w], pivots)
                done = jnp.where(row == w, rows[w], done)
        scale = lax.rsqrt(pivots)
        scaled = done * (scale * (1.5 - 0.5 * pivots * scale * scale))
        upper.append(jnp.where(jnp.logical_and(lane >= row + 8 * b, lane < 32), scaled, 0.0))
        lower.append(jnp.where(lane < 32, pltpu.roll(scaled, LANES - 32, 1), 0.0))
    return jnp.concatenate(upper, axis=0), jnp.concatenate(lower, axis=0)


def product_of_parts(left, right):
    count = len(right)
    tiles = -(-count // 4)
    rows = jnp.concatenate(left, axis=0)
    columns = jnp.concatenate(list(right) + [jnp.zeros_like(right[0])] * (4 * tiles - count), axis=0)
    blocks = lax.dot_general(
        rows, columns, (((1,), (1,)), ((), ())), preferred_element_type=jnp.float32
    )
    lane = lane_iota((SNAPS, LANES))
    folded = fold_parts([row_sum([(blocks, None)])], count)
    return tuple(jnp.where(lane < 32, value, 0.0) for value in folded)


def exact_dot(left, right, contract):
    return lax.dot_general(
        left,
        right,
        (contract, ((), ())),
        precision=lax.Precision.HIGHEST,
        preferred_element_type=jnp.float32,
    )


def modes_kernel(root, all_ref, inner_ref, edge_ref, modes_ref, factor_ref):
    lane = lane_iota((SNAPS, LANES))
    high, low = unpack_pair(add_pairs(all_ref))
    first, first_inverse = factor_and_inverse(high)
    gram_parts = [p[:, :32] for p in split_parts(high, low, row_bound(high), G_PARTS)]
    inverse_parts = [p[:, :32] for p in split_parts(first_inverse, None, row_bound(first_inverse), X_PARTS)]
    half = product_of_parts(inverse_parts, gram_parts)
    half_parts = [p[:, :32] for p in split_parts(half[0], half[1], row_bound(half[0]), G_PARTS)]
    second_gram = product_of_parts(half_parts, inverse_parts)[0]
    second, second_inverse = factor_and_inverse(second_gram)
    factor_ref[...] = exact_dot(second[:, :32], first[:, :32], ((1,), (0,))) * (1.0 / root)
    weights = exact_dot(second_inverse[:, :32], first_inverse[:, :32], ((1,), (0,))) * root
    weights = jnp.concatenate([weights] * 4, axis=1)
    pieces = []
    for _ in range(3):
        piece = weights.astype(jnp.bfloat16)
        pieces.append(piece)
        weights = weights - piece.astype(jnp.float32)
    stacked = jnp.concatenate(pieces, axis=0)

    def times(parts):
        product = jnp.dot(stacked, parts, preferred_element_type=jnp.float32)
        return (product[64:96] + product[32:64]) + product[0:32]

    sides = times(edge_ref[:, 2 * len(EDGES) * LANES :])
    ends = jnp.logical_or(lane == 0, lane == LANES - 1)
    for parts_ref, rows in ((edge_ref, EDGES), (inner_ref, INNER)):
        for index, i in enumerate(rows):
            value = times(parts_ref[:, index * 2 * LANES : (index + 1) * 2 * LANES])
            for field in range(2):
                own = value[:, field * LANES : (field + 1) * LANES]
                place = pl.ds(field * ROWS + i, SNAPS, stride=CHUNKS)
                modes_ref[place, :] = jnp.where(ends, turn(sides, -2 * (2 * i + field)), own)


def call(kernel, shapes, operands, scratch=(), flops=10**8):
    return pl.pallas_call(
        kernel,
        out_shape=shapes,
        in_specs=[pl.BlockSpec(memory_space=pltpu.VMEM)] * len(operands),
        out_specs=[pl.BlockSpec(memory_space=pltpu.VMEM)] * len(shapes),
        scratch_shapes=list(scratch),
        compiler_params=pltpu.CompilerParams(vmem_limit_bytes=8 * 2**20),
        cost_estimate=pl.CostEstimate(flops=flops, bytes_accessed=2**19, transcendentals=0),
    )(*operands)


def shards(wind_u, wind_v):
    f32 = functools.partial(jax.ShapeDtypeStruct, dtype=jnp.float32)
    bf16 = functools.partial(jax.ShapeDtypeStruct, dtype=jnp.bfloat16)
    lat_axis, lon_axis = "lat", ("z", "core")
    lat_count, lon_count = lax.axis_size(lat_axis), lax.axis_size(lon_axis)
    near, far = lax.axis_size((lat_axis, "core")), lax.axis_size("z")
    winds = jnp.stack([wind_u, wind_v]).reshape(2 * SNAPS * ROWS, LANES)

    with jax.named_scope("halo"):
        around = [(i, (i + 1) % lon_count) for i in range(lon_count)]
        back = lambda pairs: [(target, source) for source, target in pairs]
        pairing = lambda first: [(i, i + 1) for i in range(first, lat_count - 1, 2)]
        odd = jnp.full((8, LANES), lax.axis_index(lat_axis) % 2, jnp.float32)
        facing = call(rows_kernel, [f32((2 * SNAPS, LANES))] * 2, (winds, odd))
        wide, close = (
            lax.ppermute(row, lat_axis, pairing(first) + back(pairing(first)))
            for row, first in zip(facing, (1, 0))
        )

    with jax.named_scope("table"):
        step = 2.0 * math.pi / (lon_count * LANES)
        line, lane = row_iota((32, LANES)), lane_iota((32, LANES))
        first_row = lax.axis_index(lat_axis) * ROWS
        offset = jnp.where(line < 16, line - 1, jnp.where(line < 24, line - 16, (lane + 1) % LANES // 4))
        index = (first_row + offset).astype(jnp.float32)
        cosine = jnp.cos((index + 0.5 - lat_count * ROWS / 2) * step)
        table = jnp.where(line < 16, cosine, 0.5 / jnp.sqrt(cosine))

    with jax.named_scope("gram"):
        height = X_PARTS * SNAPS
        inner_parts, pair, sides = call(
            inner_kernel,
            [bf16((height, 2 * len(INNER) * LANES)), f32((2, SNAPS, LANES)), f32((SNAPS, LANES))],
            (winds, table),
            flops=2 * 10**9,
        )
        (ends,) = call(sides_kernel, [f32((SNAPS, LANES))], (winds, sides))
        low_lon = lax.ppermute(ends, lon_axis, around)
        high_lon = lax.ppermute(ends, lon_axis, back(around))
        edge_parts, gram = call(
            edge_kernel,
            [bf16((height, (2 * len(EDGES) + 1) * LANES)), f32((near * PACKED, LANES))],
            (winds, low_lon, high_lon, table, pair, sides, odd, wide, close),
        )

    def exchange(copies, axis):
        flat = copies.reshape(-1, 1, PACKED * LANES)
        return lax.all_to_all(flat, axis, 0, 0, tiled=True).reshape(copies.shape)

    with jax.named_scope("sum_near"):
        gathered = exchange(gram, (lat_axis, "core"))
        (gram,) = call(merge_kernel, [f32((far * PACKED, LANES))], (gathered,))
    with jax.named_scope("sum_far"):
        gathered = exchange(gram, "z")

    with jax.named_scope("modes"):
        root = math.sqrt(lat_count * lon_count * CHUNKS * LANES)
        modes, factor = call(
            functools.partial(modes_kernel, root),
            [f32((SNAPS * CHUNKS, LANES)), f32((SNAPS, SNAPS))],
            (gathered, inner_parts, edge_parts),
        )
    return modes.reshape(SNAPS, 2, ROWS, LANES), factor


def solution(mesh):
    lat_count, lon_count = mesh.devices.shape
    inner = Mesh(mesh.devices.reshape(lat_count, lon_count // 2, 2), ("lat", "z", "core"))
    spec = P(None, "lat", ("z", "core"))
    return jax.shard_map(
        shards,
        mesh=inner,
        in_specs=(spec, spec),
        out_specs=(P(None, None, "lat", ("z", "core")), P()),
        check_vma=False,
    )
```

```python
import functools
import math

import jax
import jax.numpy as jnp
from jax import lax
from jax.experimental import pallas as pl
from jax.experimental.pallas import tpu as pltpu
from jax.sharding import Mesh, PartitionSpec as P

SNAPS = 32
ROWS = 8
LANES = 128
CHUNKS = 2 * ROWS
X_PARTS = 4
G_PARTS = 5
PACKED = 9


def two_sum(a, b):
    total = a + b
    part = total - a
    return total, (a - (total - part)) + (b - part)


def add_terms(a, b):
    total, error = two_sum(a[0], b[0])
    for known in (a[1], b[1]):
        if known is not None:
            error = error + known
    return total, error


def add_all(terms):
    while len(terms) > 1:
        merged = [add_terms(a, b) for a, b in zip(terms[::2], terms[1::2])]
        terms = merged + terms[2 * len(merged) :]
    return terms[0]


def normalized(term):
    high = term[0] + term[1]
    return high, term[1] - (high - term[0])


def split_parts(value, low, bound, count):
    parts = []
    grid = bound * 2.0**17
    for index in range(count):
        part = (value + grid) - grid
        parts.append(part.astype(jnp.bfloat16))
        value = value - part
        if low is not None and index == 2:
            value = value + low
        grid = grid * 2.0**-8
    return parts


def lane_iota(shape):
    return lax.broadcasted_iota(jnp.int32, shape, 1)


def row_iota(shape):
    return lax.broadcasted_iota(jnp.int32, shape, 0)


def tile_row(ref, field, index):
    return ref[pl.ds(field * SNAPS * ROWS + index, SNAPS, stride=ROWS), :]


def rows_kernel(winds_ref, north_ref, south_ref):
    for field in range(2):
        place = slice(field * SNAPS, (field + 1) * SNAPS)
        north_ref[place, :] = tile_row(winds_ref, field, 0)
        south_ref[place, :] = tile_row(winds_ref, field, ROWS - 1)


def side_lanes(lane, chunk):
    return jnp.logical_or(lane == 2 * chunk, lane == (2 * chunk - 1) % LANES)


def gather_sides(values):
    lane = lane_iota((SNAPS, LANES))
    sides = jnp.zeros((SNAPS, LANES), jnp.float32)
    for chunk, value in enumerate(values):
        sides = jnp.where(side_lanes(lane, chunk), turn(value, 2 * chunk), sides)
    return sides


def sides_kernel(winds_ref, _, row_ref, sides_ref, start_ref):
    sides_ref[...] = gather_sides(
        [tile_row(winds_ref, 1 - chunk % 2, chunk // 2) for chunk in range(CHUNKS)]
    )
    start_ref[...] = row_ref[...]


def fold_parts(terms, count):
    folded = []
    for term in terms:
        for part in range(count):
            tile, group = divmod(part, 4)
            place = slice(tile * LANES, (tile + 1) * LANES)
            folded.append(tuple(None if x is None else turn(x[:, place], -32 * group) for x in term))
    return normalized(add_all(folded))


def turn(value, shift):
    return pltpu.roll(value, shift % LANES, 1) if shift % LANES else value


def row_bound(value):
    return jnp.broadcast_to(jnp.max(jnp.abs(value), axis=1, keepdims=True), value.shape)


def cut(value, bound, parts_ref, chunk):
    for part, piece in enumerate(split_parts(value, None, bound, X_PARTS)):
        parts_ref[part * SNAPS : (part + 1) * SNAPS, chunk * LANES : (chunk + 1) * LANES] = piece


def row_sum(blocks):
    groups = blocks[0][0].shape[0] // SNAPS
    return add_all(
        [
            tuple(None if x is None else x[part * SNAPS : (part + 1) * SNAPS] for x in block)
            for part in range(groups)
            for block in blocks
        ]
    )


def gram_of_parts(parts_ref):
    total = None
    for start in range(0, parts_ref.shape[1], 2 * LANES):
        piece = parts_ref[:, start : start + 2 * LANES]
        product = lax.dot_general(
            piece, piece, (((1,), (1,)), ((), ())), preferred_element_type=jnp.float32
        )
        total = (product, None) if total is None else add_terms(total, (product, None))
    return fold_parts([row_sum([total])], X_PARTS)


def tile_columns(winds_ref, low_lat_ref, high_lat_ref, table_ref, rows, sides):
    lane = lane_iota((SNAPS, LANES))
    inside = jnp.logical_and(lane > 0, lane < LANES - 1)

    def lon_diff(field, i):
        value = tile_row(winds_ref, field, i)
        after = jnp.where(lane == LANES - 1, 0.0, turn(value, -1))
        return after - jnp.where(lane == 0, 0.0, turn(value, 1))

    def weighted(field, i):
        if 0 <= i < ROWS:
            value = tile_row(winds_ref, field, i)
        else:
            value = (low_lat_ref if i < 0 else high_lat_ref)[field * SNAPS : (field + 1) * SNAPS, :]
        return table_ref[i + 1 : i + 2, :] * value

    def lat_diff(field, i):
        return weighted(field, i + 1) - weighted(field, i - 1)

    values = []
    for i in rows:
        scale = table_ref[16 + i : 17 + i, :]
        vorticity = (lon_diff(1, i) - lat_diff(0, i)) * scale
        divergence = (lon_diff(0, i) + lat_diff(1, i)) * scale
        for chunk, value in ((2 * i, vorticity), (2 * i + 1, divergence)):
            sides = jnp.where(side_lanes(lane, chunk), turn(value, 2 * chunk), sides)
            values.append(jnp.where(inside, value, 0.0))
    return values, sides


def largest_of(values):
    largest = jnp.abs(values[0])
    for value in values[1:]:
        largest = jnp.maximum(largest, jnp.abs(value))
    return row_bound(largest)


def inner_kernel(winds_ref, low_lat_ref, table_ref, parts_ref, pair_ref, sides_ref):
    none = jnp.zeros((SNAPS, LANES), jnp.float32)
    values, sides = tile_columns(winds_ref, low_lat_ref, None, table_ref, range(ROWS - 1), none)
    sides_ref[...] = sides
    bound = largest_of(values)
    for chunk, value in enumerate(values):
        cut(value, bound, parts_ref, chunk)
    pair_ref[0], pair_ref[1] = gram_of_parts(parts_ref)


def edge_kernel(
    winds_ref, low_lon_ref, high_lon_ref, table_ref, pair_ref, sides_ref, high_lat_ref, parts_ref, gram_ref
):
    lane = lane_iota((SNAPS, LANES))
    values, sides = tile_columns(winds_ref, None, high_lat_ref, table_ref, (ROWS - 1,), sides_ref[...])
    before, after = turn(low_lon_ref[...], 1), turn(high_lon_ref[...], -1)
    values.append(sides + jnp.where(lane % 2 == 0, -before, after) * table_ref[24:25, :])
    bound = largest_of(values)
    for chunk, value in enumerate(values):
        cut(value, bound, parts_ref, chunk)
    pair = normalized(add_terms(gram_of_parts(parts_ref), (pair_ref[0], pair_ref[1])))
    packed, last = pack_pair(pair)
    store_copies(gram_ref, [packed[r : r + 1, :] for r in range(8)] + [last])


def store_copies(ref, rows):
    copies = ref.shape[0] // PACKED
    for r, row in enumerate(rows):
        ref[pl.ds(r, copies, stride=PACKED), :] = jnp.broadcast_to(row[0:1, :], (copies, LANES))


def group_lane(shape):
    return lane_iota(shape) % 32


def pack_pair(pair):
    shape = (8, LANES)
    row, group = row_iota(shape), group_lane(shape)
    packed = None
    for b in range(4):
        merged = []
        for value, offset in zip(pair, (0, 16)):
            block = value[8 * b : 8 * b + 8]
            base = (8 * b - offset) % 32
            near = pltpu.roll(block, LANES - base, 1) if base else block
            block = jnp.where(row % 2 == 1, pltpu.roll(block, LANES - base - 1, 1), near)
            block = jnp.where(row % 4 >= 2, pltpu.roll(block, LANES - 2, 1), block)
            block = jnp.where(row >= 4, pltpu.roll(block, LANES - 4, 1), block)
            merged.append(block)
        block = jnp.where(group < 16, merged[0], merged[1])
        packed = block if packed is None else jnp.where(lane_iota(shape) < 32 * b, packed, block)
    half = (16, LANES)
    row, group = row_iota(half), group_lane(half)
    high = jnp.where(group == row, pltpu.roll(pair[0][:16], 16, 1), 0.0)
    low = jnp.where(group == row + 16, pair[1][:16], 0.0)
    return packed, jnp.sum(high + low, axis=0, keepdims=True)


def unpack_pair(rows):
    shape = (8, LANES)
    packed = rows[0]
    for r in range(1, 8):
        packed = jnp.where(row_iota(shape) == r, rows[r], packed)
    full = (SNAPS, LANES)
    row, lane = row_iota(full), lane_iota(full)
    distance = (lane - row) % 32
    last = jnp.concatenate([rows[8]] * 4, axis=0)
    result = []
    for offset in (0, 16):
        blocks = []
        for g in range(4):
            block = jnp.where(lane_iota(shape) < 16, pltpu.roll(packed, (-32 * g - offset) % LANES, 1), 0.0)
            blocks.append(pltpu.roll(block, 8 * g, 1, stride=1, stride_axis=0))
        right = jnp.concatenate(blocks, axis=0)
        right = jnp.where(lane < 32, right + pltpu.roll(right, LANES - 32, 1), 0.0)
        if offset:
            sides = jnp.where(row < 16, last, pltpu.roll(last, LANES - 16, 1))
        else:
            sides = jnp.where(row < 16, pltpu.roll(last, 16, 1), last)
        mirrored = jnp.concatenate([right, jnp.zeros((LANES - SNAPS, LANES), jnp.float32)], axis=0).T[:SNAPS]
        value = jnp.where(distance < 16, right, jnp.where(distance == 16, sides, mirrored))
        result.append(jnp.where(lane < 32, value, 0.0))
    return result


def add_pairs(ref):
    count = ref.shape[0] // PACKED
    group = group_lane((8, LANES))
    rows = []
    for r in range(PACKED):
        values = ref[pl.ds(r, count, stride=PACKED), :]
        if count % 8:
            values = jnp.concatenate([values, jnp.zeros((-count % 8, LANES), jnp.float32)], axis=0)
        terms = [(values[k : k + 8], None) for k in range(0, values.shape[0], 8)]
        total = add_all(terms)
        for shift in (4, 2, 1):
            other = tuple(None if x is None else pltpu.roll(x, shift, 0) for x in total)
            total = add_terms(total, other)
        low = pltpu.roll(total[0], LANES - 16, 1) + total[1]
        high = total[0] + low
        low = low - (high - total[0])
        rows.append(jnp.where(group < 16, high, pltpu.roll(low, 16, 1)))
    return rows


def merge_kernel(all_ref, out_ref):
    store_copies(out_ref, add_pairs(all_ref))


def factor_and_inverse(square):
    shape = (8, LANES)
    lane, row = lane_iota(shape), row_iota(shape)
    blocks = [
        jnp.where(lane == row + (32 + 8 * b), 1.0, square[8 * b : 8 * b + 8]) for b in range(4)
    ]
    upper, lower = [], []
    for b in range(4):
        columns = [
            [jnp.broadcast_to(block[:, 8 * b + w : 8 * b + w + 1], shape) for block in blocks[b:]]
            for w in range(8)
        ]
        rows = [jnp.broadcast_to(blocks[b][w : w + 1, :], shape) for w in range(8)]
        corner = [
            [jnp.broadcast_to(columns[t][0][w : w + 1, :], shape) if t >= w else None for t in range(8)]
            for w in range(8)
        ]
        pivots, done = corner[0][0], rows[0]
        for w in range(8):
            inverse = 1.0 / corner[w][w]
            for t in range(w + 1, 8):
                ratio = corner[w][t] * inverse
                rows[t] = rows[t] - ratio * rows[w]
                corner[t][t] = corner[t][t] - corner[w][t] * corner[w][t] * inverse
                for s in range(t + 1, 8):
                    corner[t][s] = corner[t][s] - ratio * corner[w][s]
            for i in range(1, 4 - b):
                left = columns[w][i] * inverse
                for t in range(w + 1, 8):
                    columns[t][i] = columns[t][i] - left * corner[w][t]
                blocks[b + i] = blocks[b + i] - left * rows[w]
            if w:
                pivots = jnp.where(row == w, corner[w][w], pivots)
                done = jnp.where(row == w, rows[w], done)
        scale = lax.rsqrt(pivots)
        scaled = done * (scale * (1.5 - 0.5 * pivots * scale * scale))
        upper.append(jnp.where(jnp.logical_and(lane >= row + 8 * b, lane < 32), scaled, 0.0))
        lower.append(jnp.where(lane < 32, pltpu.roll(scaled, LANES - 32, 1), 0.0))
    return jnp.concatenate(upper, axis=0), jnp.concatenate(lower, axis=0)


def product_of_parts(left, right):
    count = len(right)
    tiles = -(-count // 4)
    rows = jnp.concatenate(left, axis=0)
    columns = jnp.concatenate(list(right) + [jnp.zeros_like(right[0])] * (4 * tiles - count), axis=0)
    blocks = lax.dot_general(
        rows, columns, (((1,), (1,)), ((), ())), preferred_element_type=jnp.float32
    )
    lane = lane_iota((SNAPS, LANES))
    folded = fold_parts([row_sum([(blocks, None)])], count)
    return tuple(jnp.where(lane < 32, value, 0.0) for value in folded)


def exact_dot(left, right, contract):
    return lax.dot_general(
        left,
        right,
        (contract, ((), ())),
        precision=lax.Precision.HIGHEST,
        preferred_element_type=jnp.float32,
    )


def modes_kernel(root, all_ref, inner_ref, edge_ref, modes_ref, factor_ref):
    lane = lane_iota((SNAPS, LANES))
    high, low = unpack_pair(add_pairs(all_ref))
    first, first_inverse = factor_and_inverse(high)
    gram_parts = [p[:, :32] for p in split_parts(high, low, row_bound(high), G_PARTS)]
    inverse_parts = [p[:, :32] for p in split_parts(first_inverse, None, row_bound(first_inverse), X_PARTS)]
    half = product_of_parts(inverse_parts, gram_parts)
    half_parts = [p[:, :32] for p in split_parts(half[0], half[1], row_bound(half[0]), G_PARTS)]
    second_gram = product_of_parts(half_parts, inverse_parts)[0]
    second, second_inverse = factor_and_inverse(second_gram)
    factor_ref[...] = exact_dot(second[:, :32], first[:, :32], ((1,), (0,))) * (1.0 / root)
    weights = exact_dot(second_inverse[:, :32], first_inverse[:, :32], ((1,), (0,))) * root
    weights = jnp.concatenate([weights] * 4, axis=1)
    pieces = []
    for _ in range(3):
        piece = weights.astype(jnp.bfloat16)
        pieces.append(piece)
        weights = weights - piece.astype(jnp.float32)
    stacked = jnp.concatenate(pieces, axis=0)

    def times(parts):
        product = jnp.dot(stacked, parts, preferred_element_type=jnp.float32)
        return (product[64:96] + product[32:64]) + product[0:32]

    sides = times(edge_ref[:, 2 * LANES :])
    ends = jnp.logical_or(lane == 0, lane == LANES - 1)
    for i in range(ROWS):
        source, start = (inner_ref, i * 2 * LANES) if i < ROWS - 1 else (edge_ref, 0)
        value = times(source[:, start : start + 2 * LANES])
        for field in range(2):
            own = value[:, field * LANES : (field + 1) * LANES]
            place = pl.ds(field * ROWS + i, SNAPS, stride=CHUNKS)
            modes_ref[place, :] = jnp.where(ends, turn(sides, -2 * (2 * i + field)), own)


def call(kernel, shapes, operands, scratch=(), flops=10**8):
    return pl.pallas_call(
        kernel,
        out_shape=shapes,
        in_specs=[pl.BlockSpec(memory_space=pltpu.VMEM)] * len(operands),
        out_specs=[pl.BlockSpec(memory_space=pltpu.VMEM)] * len(shapes),
        scratch_shapes=list(scratch),
        compiler_params=pltpu.CompilerParams(vmem_limit_bytes=8 * 2**20),
        cost_estimate=pl.CostEstimate(flops=flops, bytes_accessed=2**19, transcendentals=0),
    )(*operands)


def shards(wind_u, wind_v):
    f32 = functools.partial(jax.ShapeDtypeStruct, dtype=jnp.float32)
    bf16 = functools.partial(jax.ShapeDtypeStruct, dtype=jnp.bfloat16)
    lat_axis, lon_axis = "lat", ("z", "core")
    lat_count, lon_count = lax.axis_size(lat_axis), lax.axis_size(lon_axis)
    near, far = lax.axis_size((lat_axis, "core")), lax.axis_size("z")
    winds = jnp.stack([wind_u, wind_v]).reshape(2 * SNAPS * ROWS, LANES)

    with jax.named_scope("halo"):
        up = [(i, i + 1) for i in range(lat_count - 1)]
        around = [(i, (i + 1) % lon_count) for i in range(lon_count)]
        back = lambda pairs: [(target, source) for source, target in pairs]
        north, south = call(rows_kernel, [f32((2 * SNAPS, LANES))] * 2, (winds,))
        low_lat = lax.ppermute(south, lat_axis, up)
        high_lat = lax.ppermute(north, lat_axis, back(up))
        first_row = jnp.full((8, LANES), lax.axis_index(lat_axis) * ROWS, jnp.float32)
        sides, start = call(
            sides_kernel, [f32((SNAPS, LANES)), f32((8, LANES))], (winds, low_lat, first_row)
        )
        low_lon = lax.ppermute(sides, lon_axis, around)
        high_lon = lax.ppermute(sides, lon_axis, back(around))

    with jax.named_scope("table"):
        step = 2.0 * math.pi / (lon_count * LANES)
        line, lane = row_iota((32, LANES)), lane_iota((32, LANES))
        first_row = start[0:1, :]
        offset = jnp.where(line < 16, line - 1, jnp.where(line < 24, line - 16, (lane + 1) % LANES // 4))
        index = first_row + offset.astype(jnp.float32)
        cosine = jnp.cos((index + 0.5 - lat_count * ROWS / 2) * step)
        table = jnp.where(line < 16, cosine, 0.5 / jnp.sqrt(cosine))

    with jax.named_scope("gram"):
        height = X_PARTS * SNAPS
        inner_parts, pair, sides = call(
            inner_kernel,
            [bf16((height, 2 * (ROWS - 1) * LANES)), f32((2, SNAPS, LANES)), f32((SNAPS, LANES))],
            (winds, low_lat, table),
            flops=2 * 10**9,
        )
        edge_parts, gram = call(
            edge_kernel,
            [bf16((height, 3 * LANES)), f32((near * PACKED, LANES))],
            (winds, low_lon, high_lon, table, pair, sides, high_lat),
        )

    def exchange(copies, axis):
        flat = copies.reshape(-1, 1, PACKED * LANES)
        return lax.all_to_all(flat, axis, 0, 0, tiled=True).reshape(copies.shape)

    with jax.named_scope("sum_near"):
        gathered = exchange(gram, (lat_axis, "core"))
        (gram,) = call(merge_kernel, [f32((far * PACKED, LANES))], (gathered,))
    with jax.named_scope("sum_far"):
        gathered = exchange(gram, "z")

    with jax.named_scope("modes"):
        root = math.sqrt(lat_count * lon_count * CHUNKS * LANES)
        modes, factor = call(
            functools.partial(modes_kernel, root),
            [f32((SNAPS * CHUNKS, LANES)), f32((SNAPS, SNAPS))],
            (gathered, inner_parts, edge_parts),
        )
    return modes.reshape(SNAPS, 2, ROWS, LANES), factor


def solution(mesh):
    lat_count, lon_count = mesh.devices.shape
    inner = Mesh(mesh.devices.reshape(lat_count, lon_count // 2, 2), ("lat", "z", "core"))
    spec = P(None, "lat", ("z", "core"))
    return jax.shard_map(
        shards,
        mesh=inner,
        in_specs=(spec, spec),
        out_specs=(P(None, None, "lat", ("z", "core")), P()),
        check_vma=False,
    )
```
